32 devices in a mesh: sample: 2 (over y), gx: 8 (over z, x), gy: 2 (over core).
Axes of the slice: x: 2, y: 2, z: 4, core: 2. Of those that a mesh axis runs over, the one named last changes fastest.
Arguments:
- body_force: float32 [3, 64, 32, 256], P(None, 'sample', 'gx', 'gy'), parts along dimension 1, may hold values from -36 to 36
- modulus: float32 [64, 32, 256], P('sample', 'gx', 'gy'), parts along dimension 0, may hold values from 0.12 to 8.2
Outputs:
- solution_field: float32 [3, 64, 32, 256], P(None, 'sample', 'gx', 'gy'), parts along dimension 1
- stress: float32 [6, 64, 32, 256], P(None, 'sample', 'gx', 'gy'), parts along dimension 1
The draws below stay inside these ranges and needn't reach their ends.
There are 2 independent parts, one for each index of `sample`. The reference program is written for one: setup_inputs(seed, part) draws one part's arguments, and reference() takes and returns one part's arrays. A program takes and returns all parts, laid end to end along the dimension named above; each array names one. Nothing has to cross between parts.
All inputs are finite; a program needn't handle non-finite values.
Results may differ from the reference program's by a relative error of at most 0.0039.
Values sent between devices are 32-bit elements; how exact they have to be, the bound alone decides.
A program may use at most 64 MiB of HBM per device.

```python
import math
import jax
import jax.numpy as jnp
import numpy as np
from jax import lax

EZ = 32
ITERS = 2
NX = 32
NY = 256
N_GX = 8


def draw_body_force(key, part):
    key_noise = jax.random.fold_in(key, 11)
    key_rows = jax.random.fold_in(key, 12)
    key_cols = jax.random.fold_in(key, 13)
    x_frac = jnp.arange(NX, dtype=jnp.float32) / NX
    x_ramp = jnp.exp(jnp.log(3.0) * x_frac)
    row_scale = jnp.exp(jax.random.uniform(key_rows, (NX,), jnp.float32, 0.0, jnp.log(10.0)))
    col_scale = jnp.exp(jax.random.uniform(key_cols, (NY,), jnp.float32, 0.0, jnp.log(10.0)))
    noise = jnp.clip(jax.random.normal(key_noise, (3, EZ, NX, NY), jnp.float32), -4.0, 4.0)
    scaled = 0.03 * noise * (x_ramp * row_scale)[None, None, :, None] * col_scale[None, None, None, :]
    return scaled.astype(jnp.float32)


def draw_modulus(key, part):
    key_field = jax.random.fold_in(key, 21)
    logs = 0.7 * jnp.clip(jax.random.normal(key_field, (EZ, NX, NY), jnp.float32), -3.0, 3.0)
    return jnp.exp(logs).astype(jnp.float32)


def setup_inputs(seed: int = 0, part: int = 0) -> dict:
    keys = jax.random.split(jax.random.key(seed), 3)
    own_keys = jax.random.split(jax.random.fold_in(keys[2], part), 3)
    return {
        "body_force": draw_body_force(jax.random.fold_in(jax.random.fold_in(keys[2], part), 71), part),
        "modulus": draw_modulus(jax.random.fold_in(jax.random.fold_in(keys[2], part), 71), part),
    }


def corner_list():
    return [(off_z, off_x, off_y) for off_z in (0, 1) for off_x in (0, 1) for off_y in (0, 1)]

def strain_matrix(point):
    corners = corner_list()
    grads = np.zeros((3, 8))
    for corner, offsets in enumerate(corners):
        for axis in range(3):
            value = 1.0 if offsets[axis] else -1.0
            for other in range(3):
                if other != axis:
                    value = value * (point[other] if offsets[other] else 1.0 - point[other])
            grads[axis, corner] = value
    strain = np.zeros((6, 24))
    for corner in range(8):
        for axis in range(3):
            strain[axis, axis * 8 + corner] = grads[axis, corner]
        strain[3, 0 * 8 + corner] = grads[1, corner]
        strain[3, 1 * 8 + corner] = grads[0, corner]
        strain[4, 1 * 8 + corner] = grads[2, corner]
        strain[4, 2 * 8 + corner] = grads[1, corner]
        strain[5, 0 * 8 + corner] = grads[2, corner]
        strain[5, 2 * 8 + corner] = grads[0, corner]
    return strain

def tables():
    poisson = 0.3
    lame_first = poisson / ((1.0 + poisson) * (1.0 - 2.0 * poisson))
    shear_mod = 1.0 / (2.0 * (1.0 + poisson))
    elastic = np.zeros((6, 6))
    elastic[:3, :3] = lame_first
    for axis in range(3):
        elastic[axis, axis] += 2.0 * shear_mod
        elastic[axis + 3, axis + 3] = shear_mod
    gauss_pts = [0.5 - 0.5 / math.sqrt(3.0), 0.5 + 0.5 / math.sqrt(3.0)]
    stiffness = np.zeros((24, 24))
    for first in gauss_pts:
        for second in gauss_pts:
            for third in gauss_pts:
                strain = strain_matrix((first, second, third))
                stiffness += strain.T @ elastic @ strain / 8.0
    stress_map = elastic @ strain_matrix((0.5, 0.5, 0.5))
    return (jnp.asarray(stiffness, jnp.float32), jnp.asarray(stress_map, jnp.float32))

def element_values(padded, modulus, matrix):
    z_cells, x_cells, y_cells = modulus.shape
    pieces = [padded[channel, off_z:off_z + z_cells, off_x:off_x + x_cells, off_y:off_y + y_cells] for channel in range(3) for off_z, off_x, off_y in corner_list()]
    stacked = jnp.stack(pieces)
    result = jnp.einsum('pq,qzxy->pzxy', matrix, stacked, precision=lax.Precision.HIGHEST)
    return result * modulus

def spread(values, per_corner):
    summed = None
    for corner, (off_z, off_x, off_y) in enumerate(corner_list()):
        corner_part = values[corner::8] if per_corner else values
        placed = jnp.pad(corner_part, ((0, 0), (off_z, 1 - off_z), (off_x, 1 - off_x), (off_y, 1 - off_y)))
        summed = placed if summed is None else summed + placed
    return summed

def assemble(field_in, modulus, matrix, per_corner):
    z_cells, x_total, y_total = modulus.shape
    block_width = x_total // N_GX
    padded = jnp.pad(field_in, ((0, 0), (1, 0), (1, 0), (1, 0)))

    def block_at(block_index):
        block_start = block_index * block_width
        padded_block = lax.dynamic_slice_in_dim(padded, block_start, block_width + 1, 2)
        modulus_block = lax.dynamic_slice_in_dim(modulus, block_start, block_width, 1)
        return spread(element_values(padded_block, modulus_block, matrix), per_corner)
    blocks = lax.map(block_at, jnp.arange(N_GX, dtype=jnp.int32))
    channels = blocks.shape[1]
    main_rows = jnp.transpose(blocks[:, :, :, :block_width, :], (1, 2, 0, 3, 4))
    main_rows = main_rows.reshape(channels, z_cells + 1, x_total, y_total + 1)
    assembled = jnp.pad(main_rows, ((0, 0), (0, 0), (0, 1), (0, 0)))
    tail_rows = jnp.transpose(blocks[:, :, :, block_width, :], (1, 2, 0, 3))
    assembled = assembled.at[:, :, block_width::block_width, :].add(tail_rows)
    return assembled[:, 1:, 1:, 1:]

def node_factor(cells):
    nodes = jnp.arange(1, cells + 1, dtype=jnp.int32)
    return jnp.where(nodes < cells, jnp.float32(2.0), jnp.float32(1.0))

def reference(body_force, modulus):
    stiffness, stress_map = tables()
    z_cells, x_total, y_total = modulus.shape
    solution_field = jnp.zeros_like(body_force)
    residual = body_force
    direction = body_force
    norm_now = jnp.sum(residual * residual)
    for iteration in range(ITERS):
        image_vec = assemble(direction, modulus, stiffness, True)
        step_len = norm_now / jnp.sum(direction * image_vec)
        solution_field = solution_field + step_len * direction
        residual = residual - step_len * image_vec
        norm_next = jnp.sum(residual * residual)
        direction = residual + norm_next / norm_now * direction
        norm_now = norm_next
    summed = assemble(solution_field, modulus, stress_map, False)
    counts = node_factor(z_cells)[:, None, None] * node_factor(x_total)[None, :, None] * node_factor(y_total)[None, None, :]
    stress = summed / counts
    return (solution_field, stress)
```

```python
import functools
import math

import jax
import jax.numpy as jnp
import numpy as np
from jax import lax
from jax.experimental import pallas as pl
from jax.experimental.pallas import tpu as pltpu
from jax.sharding import PartitionSpec as P

MESH = pl.DeviceIdType.MESH


def corner_list():
    return [(off_z, off_x, off_y) for off_z in (0, 1) for off_x in (0, 1) for off_y in (0, 1)]


def strain_matrix(point):
    corners = corner_list()
    grads = np.zeros((3, 8))
    for corner, offsets in enumerate(corners):
        for axis in range(3):
            value = 1.0 if offsets[axis] else -1.0
            for other in range(3):
                if other != axis:
                    value = value * (point[other] if offsets[other] else 1.0 - point[other])
            grads[axis, corner] = value
    strain = np.zeros((6, 24))
    for corner in range(8):
        for axis in range(3):
            strain[axis, axis * 8 + corner] = grads[axis, corner]
        strain[3, 0 * 8 + corner] = grads[1, corner]
        strain[3, 1 * 8 + corner] = grads[0, corner]
        strain[4, 1 * 8 + corner] = grads[2, corner]
        strain[4, 2 * 8 + corner] = grads[1, corner]
        strain[5, 0 * 8 + corner] = grads[2, corner]
        strain[5, 2 * 8 + corner] = grads[0, corner]
    return strain


def modal_tables():
    poisson = 0.3
    lame_first = poisson / ((1.0 + poisson) * (1.0 - 2.0 * poisson))
    shear_mod = 1.0 / (2.0 * (1.0 + poisson))
    elastic = np.zeros((6, 6))
    elastic[:3, :3] = lame_first
    for axis in range(3):
        elastic[axis, axis] += 2.0 * shear_mod
        elastic[axis + 3, axis + 3] = shear_mod
    gauss_pts = [0.5 - 0.5 / math.sqrt(3.0), 0.5 + 0.5 / math.sqrt(3.0)]
    stiffness = np.zeros((24, 24))
    for first in gauss_pts:
        for second in gauss_pts:
            for third in gauss_pts:
                strain = strain_matrix((first, second, third))
                stiffness += strain.T @ elastic @ strain / 8.0
    stress_map = elastic @ strain_matrix((0.5, 0.5, 0.5))
    pair = np.array([[1.0, 1.0], [-1.0, 1.0]])
    modes = np.kron(np.eye(3), np.kron(pair, np.kron(pair, pair)))
    stiffness = modes @ stiffness @ modes.T / 64.0
    stress_map = stress_map @ modes.T / 8.0

    def rows_of(matrix):
        out = []
        for row in matrix:
            terms = [(q // 8, (q % 8) // 4, (q % 4) // 2, q % 2, float(v)) for q, v in enumerate(row) if abs(v) > 1e-9]
            out.append(terms)
        return out

    return rows_of(stiffness), rows_of(stress_map)


STIFF, STRESS = modal_tables()
B_RIGHT, P_RIGHT, S_RIGHT, D_RIGHT, B_LEFT, E_LEFT, Q_LEFT, S_LEFT, D_LEFT, S_OTHER = range(10)


def combine(terms, fields):
    total = None
    for c, a, b, d, value in terms:
        part = fields[c][a, b, d] * np.float32(value)
        total = part if total is None else total + part
    return total


def kernel(n_gx, n_gy, f_hbm, e_hbm, x_out, s_out,
           f_in, e_in, b_ref, e_ref, bl, pp, br, er, qq, p_out, q_out,
           msg, st_same, st_other, w_ref, ws_ref, bs_ref, sb_ref, sw_ref, ssb_ref, ssw_ref,
           red, slots, in_sem, send_sem, recv_sem, red_send, red_recv):
    gx, gy = lax.axis_index("gx"), lax.axis_index("gy")
    rows = e_hbm.shape[0]
    planes, depth, width = b_ref.shape[0], b_ref.shape[2], b_ref.shape[3]
    has_left, has_right = gx > 0, gx < n_gx - 1
    other = 1 - gy
    n = n_gx * n_gy
    me = gx * n_gy + gy

    load_f = pltpu.make_async_copy(f_hbm, f_in, in_sem.at[0])
    load_e = pltpu.make_async_copy(e_hbm, e_in, in_sem.at[1])
    load_f.start()
    load_e.start()

    barrier = pltpu.get_barrier_semaphore()

    def member(k):
        target = lax.rem(me + k, n)
        return {"gx": target // n_gy, "gy": lax.rem(target, n_gy)}

    def each_member(body):
        if n <= 32:
            for k in range(1, n):
                body(k)
        else:
            lax.fori_loop(1, n, lambda k, carry: (body(k), carry)[1], 0)

    each_member(lambda k: pl.semaphore_signal(barrier, inc=1, device_id=member(k), device_id_type=MESH))

    shape = (depth, width)
    lane = lax.broadcasted_iota(jnp.int32, shape, 1)
    row = lax.broadcasted_iota(jnp.int32, shape, 0)
    zero = jnp.zeros(shape, jnp.float32)
    first_row, last_row = row == 0, row == depth - 1
    first_lane, last_lane = lane == 0, lane == width - 1

    @pl.when(gx == 0)
    def _():
        bl[...] = jnp.zeros_like(bl)
        pp[...] = jnp.zeros_like(pp)
        st_same[0] = zero
        st_other[0] = zero

    @pl.when(gx == n_gx - 1)
    def _():
        br[...] = jnp.zeros_like(br)
        er[...] = jnp.zeros_like(er)
        qq[...] = jnp.zeros_like(qq)
        st_same[1] = zero
        st_other[3] = zero

    def remote(src, dst, which, x, y):
        return pltpu.make_async_remote_copy(
            src_ref=src, dst_ref=dst, send_sem=send_sem.at[which], recv_sem=recv_sem.at[which],
            device_id={"gx": x, "gy": y}, device_id_type=MESH)

    right, left = lax.rem(gx + 1, n_gx), lax.rem(gx + n_gx - 1, n_gx)
    to_right = {
        B_RIGHT: remote(b_ref.at[planes - 1], bl, B_RIGHT, right, gy),
        P_RIGHT: remote(p_out, pp, P_RIGHT, right, gy),
        S_RIGHT: remote(msg.at[1], st_same.at[0], S_RIGHT, right, gy),
        D_RIGHT: remote(msg.at[1], st_other.at[0], D_RIGHT, right, other),
    }
    to_left = {
        B_LEFT: remote(b_ref.at[0], br, B_LEFT, left, gy),
        E_LEFT: remote(e_ref.at[0], er, E_LEFT, left, gy),
        Q_LEFT: remote(q_out, qq, Q_LEFT, left, gy),
        S_LEFT: remote(msg.at[0], st_same.at[1], S_LEFT, left, gy),
        D_LEFT: remote(msg.at[0], st_other.at[3], D_LEFT, left, other),
    }
    to_other = remote(msg, st_other.at[pl.ds(1, 2)], S_OTHER, gx, other)

    def start(rights, lefts):
        @pl.when(has_right)
        def _():
            for which in rights:
                to_right[which].start()

        @pl.when(has_left)
        def _():
            for which in lefts:
                to_left[which].start()

    def arrived(rights, lefts):
        @pl.when(has_left)
        def _():
            for which in rights:
                to_right[which].wait_recv()

        @pl.when(has_right)
        def _():
            for which in lefts:
                to_left[which].wait_recv()

    load_f.wait()
    load_e.wait()
    for p in range(planes):
        for c in range(3):
            b_ref[p, c] = f_in[c, pl.ds(p, depth, stride=planes), :]
        e_ref[p] = e_in[pl.ds(p, depth, stride=planes), :]

    pl.semaphore_wait(barrier, n - 1)
    start([B_RIGHT], [B_LEFT, E_LEFT])

    for side in range(2):
        packed = None
        for c in range(4):
            for t in range(2):
                p = 2 * side + t
                value = b_ref[p, c] if c < 3 else e_ref[p]
                turned = pltpu.roll(value, (32 * c + 16 * t + 8) % width, 1)
                packed = turned if packed is None else jnp.where(lane // 16 == 2 * c + t, turned, packed)
        msg[side] = packed
    to_other.start()
    start([S_RIGHT, D_RIGHT], [S_LEFT, D_LEFT])

    def y_below(value, edge):
        value = pltpu.roll(value, 1, 1)
        return jnp.where(first_lane, 0.0, value) if edge else value

    def y_above(value, edge):
        value = pltpu.roll(value, width - 1, 1)
        return jnp.where(last_lane, 0.0, value) if edge else value

    def z_below(value):
        return jnp.where(first_row, 0.0, pltpu.roll(value, 1, 0))

    def z_above(value):
        return jnp.where(last_row, 0.0, pltpu.roll(value, depth - 1, 0))

    def forward(value, edge):
        below = y_below(value, edge)
        out = {}
        for d, part in ((0, value + below), (1, value - below)):
            low = z_below(part)
            out[0, d], out[1, d] = part + low, part - low
        return out

    def pair_up(low, high):
        fields = []
        for c in range(3):
            field = {}
            for key in high[c]:
                a, d = key
                field[a, 0, d] = high[c][key] + low[c][key]
                field[a, 1, d] = high[c][key] - low[c][key]
            fields.append(field)
        return fields

    def forces(fields, scale):
        highs, lows = [], []
        for c in range(3):
            high, low = {}, {}
            for a in range(2):
                for d in range(2):
                    diff = combine(STIFF[c * 8 + 4 * a + 2 + d], fields) * scale
                    terms = STIFF[c * 8 + 4 * a + d]
                    if terms:
                        same = combine(terms, fields) * scale
                        high[a, d], low[a, d] = same + diff, same - diff
                    else:
                        high[a, d], low[a, d] = diff, -diff
            highs.append(high)
            lows.append(low)
        return highs, lows

    def back(modes, edge):
        parts = []
        for d in range(2):
            parts.append(modes[0, d] + modes[1, d] + z_above(modes[0, d] - modes[1, d]))
        return parts[0] + parts[1] + y_above(parts[0] - parts[1], edge)

    def add(first, second):
        return {key: first[key] + second[key] for key in first}

    def energy(fields, scale):
        total = None
        for c in range(3):
            for k in range(1, 8):
                part = combine(STIFF[c * 8 + k], fields) * fields[c][k // 4, (k % 4) // 2, k % 2]
                total = part if total is None else total + part
        return total * scale

    def stresses(fields, scale):
        return [combine(STRESS[r], fields) * scale for r in range(6)]

    def spread(value, edge):
        value = value + z_above(value)
        return value + y_above(value, edge)

    def b_plane(p, c):
        return bl[c] if p < 0 else br[c] if p >= planes else b_ref[p, c]

    def b_modes(p):
        return [forward(b_plane(p, c), True) for c in range(3)]

    m2 = [b_modes(p) for p in range(planes)]
    highs, lows, s_b = {}, {}, {}

    def do_element(p, low, high):
        scale = er[...] if p >= planes else e_ref[p]
        fields = pair_up(low, high)
        highs[p], lows[p] = forces(fields, scale)
        s_b[p] = stresses(fields, scale)

    do_element(planes - 1, m2[planes - 2], m2[planes - 1])
    for c in range(3):
        p_out[c] = back(highs[planes - 1][c], True)
    do_element(1, m2[0], m2[1])
    for c in range(3):
        q_out[c] = back(lows[1][c], True)
    start([P_RIGHT], [Q_LEFT])
    for p in range(2, planes - 1):
        do_element(p, m2[p - 1], m2[p])
    for p in range(1, planes - 1):
        for c in range(3):
            w_ref[p + 1, c] = back(add(highs[p][c], lows[p + 1][c]), True)
        if p > 1:
            pass
    for p in range(1, planes - 1):
        for r in range(6):
            sb_ref[p, r] = spread(s_b[p][r] + s_b[p + 1][r], True)

    to_other.wait_recv()
    arrived([S_RIGHT, D_RIGHT], [S_LEFT, D_LEFT])
    mine = lax.rem(lane, 16) // 8 == gy
    quarters = [
        jnp.where(mine, st_same[0], st_other[0]),
        jnp.where(mine, msg[0], st_other[1]),
        jnp.where(mine, msg[1], st_other[2]),
        jnp.where(mine, st_same[1], st_other[3]),
    ]
    strip = []
    for c in range(4):
        total = None
        for q in range(4):
            turn = (32 * (q - c)) % width
            turned = pltpu.roll(quarters[q], turn, 1) if turn else quarters[q]
            total = turned if total is None else jnp.where(lane // 32 == q, turned, total)
        strip.append(total)
    strip_e = strip[3]

    def strip_fields(values):
        high = [forward(value, False) for value in values]
        low = [{key: pltpu.roll(field[key], 16, 1) for key in field} for field in high]
        return pair_up(low, high)

    def next_slot(value):
        return pltpu.roll(value, width - 16, 1)

    fields = strip_fields(strip[:3])
    strip_high, strip_low = forces(fields, strip_e)
    s_strip = stresses(fields, strip_e)
    clamped = jnp.logical_and(gx == 0, lane < 32)
    strip_w = []
    for c in range(3):
        modes = {key: strip_high[c][key] + next_slot(strip_low[c][key]) for key in strip_high[c]}
        strip_w.append(jnp.where(clamped, 0.0, back(modes, False)))
    for r in range(6):
        ssb_ref[r] = spread(s_strip[r] + next_slot(s_strip[r]), False)

    at_cut = lane == (width - 1) * other

    def mend(value, strip_value, p):
        turn = (-(16 * (p + 2) + 8)) % width
        turned = pltpu.roll(strip_value, turn, 1) if turn else strip_value
        return jnp.where(at_cut, turned, value)

    arrived([B_RIGHT], [B_LEFT, E_LEFT])
    modes_l, modes_r = b_modes(-1), b_modes(planes)
    do_element(0, modes_l, m2[0])
    do_element(planes, m2[planes - 1], modes_r)
    for p in (0, planes - 1):
        for c in range(3):
            w_ref[p + 1, c] = back(add(highs[p][c], lows[p + 1][c]), True)
        for r in range(6):
            sb_ref[p, r] = spread(s_b[p][r] + s_b[p + 1][r], True)
    arrived([P_RIGHT], [Q_LEFT])
    for c in range(3):
        w_ref[0, c] = jnp.where(gx == 0, 0.0, pp[c] + back(lows[0][c], True))
        w_ref[planes + 1, c] = qq[c] + back(highs[planes][c], True)
    for p in range(-1, planes + 1):
        for c in range(3):
            w_ref[p + 1, c] = mend(w_ref[p + 1, c], strip_w[c], p)

    sum_bb, sum_bw, sum_ww, sum_wkw = zero, zero, zero, zero
    for p in range(planes):
        for c in range(3):
            b, w = b_ref[p, c], w_ref[p + 1, c]
            sum_bb = sum_bb + b * b
            sum_bw = sum_bw + b * w
            sum_ww = sum_ww + w * w
    s_w = {}
    low = [forward(w_ref[0, c], True) for c in range(3)]
    for p in range(planes + 1):
        high = [forward(w_ref[p + 1, c], True) for c in range(3)]
        scale = er[...] if p >= planes else e_ref[p]
        fields = pair_up(low, high)
        if p < planes:
            sum_wkw = sum_wkw + energy(fields, scale)
        s_w[p] = stresses(fields, scale)
        low = high
    sum_wkw = jnp.where(jnp.logical_and(first_lane, gy == 1), 0.0, sum_wkw)
    fields = strip_fields(strip_w)
    s_strip = stresses(fields, strip_e)
    counted = jnp.logical_and(lax.rem(lane, 16) == 8, jnp.logical_and(lane >= 32, lane < 32 + 16 * planes))
    counted = jnp.logical_and(counted, gy == 1)
    sum_wkw = sum_wkw + jnp.where(counted, energy(fields, strip_e), 0.0)

    row8 = lax.broadcasted_iota(jnp.int32, (8, width), 0)
    partial = jnp.zeros((8, width), jnp.float32)
    for k, total in enumerate((sum_bb, sum_bw, sum_ww, sum_wkw)):
        partial = jnp.where(row8 == k, jnp.sum(total, axis=0, keepdims=True), partial)
    red[...] = partial

    def send_sum(k):
        pltpu.make_async_remote_copy(
            src_ref=red, dst_ref=slots.at[k - 1], send_sem=red_send, recv_sem=red_recv,
            device_id=member(k), device_id_type=MESH).start()

    each_member(send_sum)

    for r in range(6):
        ssw_ref[r] = spread(s_strip[r] + next_slot(s_strip[r]), False)
    z_share = jnp.where(last_row, 1.0, 0.5)
    yz_share = z_share * jnp.where(jnp.logical_and(last_lane, gy == n_gy - 1), 1.0, 0.5)
    for p in range(planes):
        share = yz_share * 0.5
        if p == planes - 1:
            share = jnp.where(has_right, share, yz_share)
        for r in range(6):
            value = spread(s_w[p][r] + s_w[p + 1][r], True)
            sw_ref[p, r] = mend(value, ssw_ref[r], p) * share
            sb_ref[p, r] = mend(sb_ref[p, r], ssb_ref[r], p) * share

    pltpu.make_async_copy(slots, slots, red_recv).wait()
    total = red[...]
    if n <= 32:
        for k in range(n - 1):
            total = total + slots[k]
    else:
        total = lax.fori_loop(0, n - 1, lambda k, value: value + slots[k], total)
    sums = jnp.broadcast_to(jnp.sum(total, axis=1, keepdims=True), (8, width))
    bb, bw, ww, wkw = (sums[k : k + 1] for k in range(4))
    first_step = bb / bw
    norm = bb - 2.0 * first_step * bw + first_step * first_step * ww
    ratio = norm / bb
    grown = 1.0 + ratio
    curve = grown * grown * bw - 2.0 * grown * first_step * ww + first_step * first_step * wkw
    second_step = norm / curve
    on_b = first_step + second_step * grown
    on_w = -second_step * first_step
    for p in range(planes):
        for c in range(3):
            x_out[c, pl.ds(p, depth, stride=planes), :] = on_b * b_ref[p, c] + on_w * w_ref[p + 1, c]
        for r in range(6):
            s_out[r, pl.ds(p, depth, stride=planes), :] = on_b * sb_ref[p, r] + on_w * sw_ref[p, r]

    to_other.wait_send()
    pltpu.make_async_copy(slots, slots, red_send).wait()

    @pl.when(has_right)
    def _():
        for copy in to_right.values():
            copy.wait_send()

    @pl.when(has_left)
    def _():
        for copy in to_left.values():
            copy.wait_send()


def solution(mesh):
    n_gx, n_gy = mesh.shape["gx"], mesh.shape["gy"]

    def per_device(body_force, modulus):
        depth, planes, width = modulus.shape
        assert n_gy == 2 and planes == 4 and width == 128
        rows = depth * planes
        n = n_gx * n_gy
        plane = (depth, width)
        vmem = lambda *dims: pltpu.VMEM(dims, jnp.float32)
        field, stress = pl.pallas_call(
            functools.partial(kernel, n_gx, n_gy),
            out_shape=(
                jax.ShapeDtypeStruct((3, rows, width), jnp.float32),
                jax.ShapeDtypeStruct((6, rows, width), jnp.float32),
            ),
            in_specs=[pl.BlockSpec(memory_space=pl.ANY)] * 2,
            out_specs=(pl.BlockSpec(memory_space=pltpu.VMEM),) * 2,
            scratch_shapes=[
                vmem(3, rows, width),
                vmem(rows, width),
                vmem(planes, 3, *plane),
                vmem(planes, *plane),
                vmem(3, *plane),
                vmem(3, *plane),
                vmem(3, *plane),
                vmem(*plane),
                vmem(3, *plane),
                vmem(3, *plane),
                vmem(3, *plane),
                vmem(2, *plane),
                vmem(2, *plane),
                vmem(4, *plane),
                vmem(planes + 2, 3, *plane),
                vmem(3, *plane),
                vmem(3, *plane),
                vmem(planes, 6, *plane),
                vmem(planes, 6, *plane),
                vmem(6, *plane),
                vmem(6, *plane),
                vmem(8, width),
                vmem(n - 1, 8, width),
                pltpu.SemaphoreType.DMA((2,)),
                pltpu.SemaphoreType.DMA((10,)),
                pltpu.SemaphoreType.DMA((10,)),
                pltpu.SemaphoreType.DMA,
                pltpu.SemaphoreType.DMA,
            ],
            compiler_params=pltpu.CompilerParams(
                collective_id=0, has_side_effects=True, vmem_limit_bytes=32 * 1024 * 1024
            ),
        )(body_force.reshape(3, rows, width), modulus.reshape(rows, width))
        return (
            field.reshape(3, depth, planes, width),
            stress.reshape(6, depth, planes, width),
        )

    return jax.shard_map(
        per_device,
        mesh=mesh,
        in_specs=(P(None, "sample", "gx", "gy"), P("sample", "gx", "gy")),
        out_specs=(P(None, "sample", "gx", "gy"), P(None, "sample", "gx", "gy")),
        check_vma=False,
    )
```

```python
import functools
import math

import jax
import jax.numpy as jnp
import numpy as np
from jax import lax
from jax.experimental import pallas as pl
from jax.experimental.pallas import tpu as pltpu
from jax.sharding import PartitionSpec as P

MESH = pl.DeviceIdType.MESH


def corner_list():
    return [(off_z, off_x, off_y) for off_z in (0, 1) for off_x in (0, 1) for off_y in (0, 1)]


def strain_matrix(point):
    corners = corner_list()
    grads = np.zeros((3, 8))
    for corner, offsets in enumerate(corners):
        for axis in range(3):
            value = 1.0 if offsets[axis] else -1.0
            for other in range(3):
                if other != axis:
                    value = value * (point[other] if offsets[other] else 1.0 - point[other])
            grads[axis, corner] = value
    strain = np.zeros((6, 24))
    for corner in range(8):
        for axis in range(3):
            strain[axis, axis * 8 + corner] = grads[axis, corner]
        strain[3, 0 * 8 + corner] = grads[1, corner]
        strain[3, 1 * 8 + corner] = grads[0, corner]
        strain[4, 1 * 8 + corner] = grads[2, corner]
        strain[4, 2 * 8 + corner] = grads[1, corner]
        strain[5, 0 * 8 + corner] = grads[2, corner]
        strain[5, 2 * 8 + corner] = grads[0, corner]
    return strain


def modal_tables():
    poisson = 0.3
    lame_first = poisson / ((1.0 + poisson) * (1.0 - 2.0 * poisson))
    shear_mod = 1.0 / (2.0 * (1.0 + poisson))
    elastic = np.zeros((6, 6))
    elastic[:3, :3] = lame_first
    for axis in range(3):
        elastic[axis, axis] += 2.0 * shear_mod
        elastic[axis + 3, axis + 3] = shear_mod
    gauss_pts = [0.5 - 0.5 / math.sqrt(3.0), 0.5 + 0.5 / math.sqrt(3.0)]
    stiffness = np.zeros((24, 24))
    for first in gauss_pts:
        for second in gauss_pts:
            for third in gauss_pts:
                strain = strain_matrix((first, second, third))
                stiffness += strain.T @ elastic @ strain / 8.0
    stress_map = elastic @ strain_matrix((0.5, 0.5, 0.5))
    pair = np.array([[1.0, 1.0], [-1.0, 1.0]])
    modes = np.kron(np.eye(3), np.kron(pair, np.kron(pair, pair)))
    stiffness = modes @ stiffness @ modes.T / 64.0
    stress_map = stress_map @ modes.T / 8.0

    def rows_of(matrix):
        out = []
        for row in matrix:
            terms = [(q // 8, (q % 8) // 4, (q % 4) // 2, q % 2, float(v)) for q, v in enumerate(row) if abs(v) > 1e-9]
            out.append(terms)
        return out

    return rows_of(stiffness), rows_of(stress_map)


STIFF, STRESS = modal_tables()
B_RIGHT, P_RIGHT, S_RIGHT, D_RIGHT, B_LEFT, E_LEFT, Q_LEFT, S_LEFT, D_LEFT, S_OTHER = range(10)


def combine(terms, fields):
    total = None
    for c, a, b, d, value in terms:
        part = fields[c][a, b, d] * np.float32(value)
        total = part if total is None else total + part
    return total


def kernel(n_gx, n_gy, f_hbm, e_hbm, x_out, s_out,
           f_in, e_in, b_ref, e_ref, bl, pp, br, er, qq, p_out, q_out,
           msg, st_same, st_other, w_ref, sb_ref, sw_ref, ssb_ref, ssw_ref,
           red, slots, in_sem, send_sem, recv_sem, red_send, red_recv):
    gx, gy = lax.axis_index("gx"), lax.axis_index("gy")
    rows = e_hbm.shape[0]
    planes, depth, width = b_ref.shape[0], b_ref.shape[2], b_ref.shape[3]
    has_left, has_right = gx > 0, gx < n_gx - 1
    other = 1 - gy
    n = n_gx * n_gy
    me = gx * n_gy + gy

    load_f = pltpu.make_async_copy(f_hbm, f_in, in_sem.at[0])
    load_e = pltpu.make_async_copy(e_hbm, e_in, in_sem.at[1])
    load_f.start()
    load_e.start()

    barrier = pltpu.get_barrier_semaphore()

    def member(k):
        target = lax.rem(me + k, n)
        return {"gx": target // n_gy, "gy": lax.rem(target, n_gy)}

    def each_member(body):
        if n <= 32:
            for k in range(1, n):
                body(k)
        else:
            lax.fori_loop(1, n, lambda k, carry: (body(k), carry)[1], 0)

    each_member(lambda k: pl.semaphore_signal(barrier, inc=1, device_id=member(k), device_id_type=MESH))

    shape = (depth, width)
    lane = lax.broadcasted_iota(jnp.int32, shape, 1)
    row = lax.broadcasted_iota(jnp.int32, shape, 0)
    zero = jnp.zeros(shape, jnp.float32)
    first_row, last_row = row == 0, row == depth - 1
    first_lane, last_lane = lane == 0, lane == width - 1

    @pl.when(gx == 0)
    def _():
        bl[...] = jnp.zeros_like(bl)
        pp[...] = jnp.zeros_like(pp)
        st_same[0] = zero
        st_other[0] = zero

    @pl.when(gx == n_gx - 1)
    def _():
        br[...] = jnp.zeros_like(br)
        er[...] = jnp.zeros_like(er)
        qq[...] = jnp.zeros_like(qq)
        st_same[1] = zero
        st_other[3] = zero

    def remote(src, dst, which, x, y):
        return pltpu.make_async_remote_copy(
            src_ref=src, dst_ref=dst, send_sem=send_sem.at[which], recv_sem=recv_sem.at[which],
            device_id={"gx": x, "gy": y}, device_id_type=MESH)

    right, left = lax.rem(gx + 1, n_gx), lax.rem(gx + n_gx - 1, n_gx)
    to_right = {
        B_RIGHT: remote(b_ref.at[planes - 1], bl, B_RIGHT, right, gy),
        P_RIGHT: remote(p_out, pp, P_RIGHT, right, gy),
        S_RIGHT: remote(msg.at[1], st_same.at[0], S_RIGHT, right, gy),
        D_RIGHT: remote(msg.at[1], st_other.at[0], D_RIGHT, right, other),
    }
    to_left = {
        B_LEFT: remote(b_ref.at[0], br, B_LEFT, left, gy),
        E_LEFT: remote(e_ref.at[0], er, E_LEFT, left, gy),
        Q_LEFT: remote(q_out, qq, Q_LEFT, left, gy),
        S_LEFT: remote(msg.at[0], st_same.at[1], S_LEFT, left, gy),
        D_LEFT: remote(msg.at[0], st_other.at[3], D_LEFT, left, other),
    }
    to_other = remote(msg, st_other.at[pl.ds(1, 2)], S_OTHER, gx, other)

    def start(rights, lefts):
        @pl.when(has_right)
        def _():
            for which in rights:
                to_right[which].start()

        @pl.when(has_left)
        def _():
            for which in lefts:
                to_left[which].start()

    def arrived(rights, lefts):
        @pl.when(has_left)
        def _():
            for which in rights:
                to_right[which].wait_recv()

        @pl.when(has_right)
        def _():
            for which in lefts:
                to_left[which].wait_recv()

    def take(p):
        for c in range(3):
            b_ref[p, c] = f_in[c, pl.ds(p, depth, stride=planes), :]
        e_ref[p] = e_in[pl.ds(p, depth, stride=planes), :]

    load_f.wait()
    load_e.wait()
    take(planes - 1)
    take(0)
    pl.semaphore_wait(barrier, n - 1)
    start([B_RIGHT], [B_LEFT, E_LEFT])
    for p in range(1, planes - 1):
        take(p)

    for side in range(2):
        packed = None
        for c in range(4):
            for t in range(2):
                p = 2 * side + t
                value = b_ref[p, c] if c < 3 else e_ref[p]
                turned = pltpu.roll(value, (32 * c + 16 * t + 8) % width, 1)
                packed = turned if packed is None else jnp.where(lane // 16 == 2 * c + t, turned, packed)
        msg[side] = packed
    to_other.start()
    start([S_RIGHT, D_RIGHT], [S_LEFT, D_LEFT])

    def y_below(value, edge):
        value = pltpu.roll(value, 1, 1)
        return jnp.where(first_lane, 0.0, value) if edge else value

    def y_above(value, edge):
        value = pltpu.roll(value, width - 1, 1)
        return jnp.where(last_lane, 0.0, value) if edge else value

    def z_below(value):
        return jnp.where(first_row, 0.0, pltpu.roll(value, 1, 0))

    def z_above(value):
        return jnp.where(last_row, 0.0, pltpu.roll(value, depth - 1, 0))

    def forward(value, edge):
        below = y_below(value, edge)
        out = {}
        for d, part in ((0, value + below), (1, value - below)):
            low = z_below(part)
            out[0, d], out[1, d] = part + low, part - low
        return out

    def pair_up(low, high):
        fields = []
        for c in range(3):
            field = {}
            for key in high[c]:
                a, d = key
                field[a, 0, d] = high[c][key] + low[c][key]
                field[a, 1, d] = high[c][key] - low[c][key]
            fields.append(field)
        return fields

    def forces(fields, scale):
        highs, lows = [], []
        for c in range(3):
            high, low = {}, {}
            for a in range(2):
                for d in range(2):
                    diff = combine(STIFF[c * 8 + 4 * a + 2 + d], fields) * scale
                    terms = STIFF[c * 8 + 4 * a + d]
                    if terms:
                        same = combine(terms, fields) * scale
                        high[a, d], low[a, d] = same + diff, same - diff
                    else:
                        high[a, d], low[a, d] = diff, -diff
            highs.append(high)
            lows.append(low)
        return highs, lows

    def back(modes, edge):
        parts = []
        for d in range(2):
            parts.append(modes[0, d] + modes[1, d] + z_above(modes[0, d] - modes[1, d]))
        return parts[0] + parts[1] + y_above(parts[0] - parts[1], edge)

    def add(first, second):
        return {key: first[key] + second[key] for key in first}

    def energy(fields, scale):
        total = None
        for c in range(3):
            for k in range(1, 8):
                part = combine(STIFF[c * 8 + k], fields) * fields[c][k // 4, (k % 4) // 2, k % 2]
                total = part if total is None else total + part
        return total * scale

    def stresses(fields, scale):
        return [combine(STRESS[r], fields) * scale for r in range(6)]

    def spread(value, edge):
        value = value + z_above(value)
        return value + y_above(value, edge)

    def b_plane(p, c):
        return bl[c] if p < 0 else br[c] if p >= planes else b_ref[p, c]

    def b_modes(p):
        return [forward(b_plane(p, c), True) for c in range(3)]

    m2 = [b_modes(p) for p in range(planes)]
    highs, lows, s_b = {}, {}, {}

    def do_element(p, low, high):
        scale = er[...] if p >= planes else e_ref[p]
        fields = pair_up(low, high)
        highs[p], lows[p] = forces(fields, scale)
        s_b[p] = stresses(fields, scale)

    do_element(planes - 1, m2[planes - 2], m2[planes - 1])
    for c in range(3):
        p_out[c] = back(highs[planes - 1][c], True)
    do_element(1, m2[0], m2[1])
    for c in range(3):
        q_out[c] = back(lows[1][c], True)
    start([P_RIGHT], [Q_LEFT])
    for p in range(2, planes - 1):
        do_element(p, m2[p - 1], m2[p])

    def raw_w(p):
        for c in range(3):
            w_ref[p + 1, c] = back(add(highs[p][c], lows[p + 1][c]), True)

    for p in range(1, planes - 1):
        raw_w(p)

    to_other.wait_recv()
    arrived([S_RIGHT, D_RIGHT], [S_LEFT, D_LEFT])
    mine = lax.rem(lane, 16) // 8 == gy
    quarters = [
        jnp.where(mine, st_same[0], st_other[0]),
        jnp.where(mine, msg[0], st_other[1]),
        jnp.where(mine, msg[1], st_other[2]),
        jnp.where(mine, st_same[1], st_other[3]),
    ]
    strip = []
    for c in range(4):
        total = None
        for q in range(4):
            turn = (32 * (q - c)) % width
            turned = pltpu.roll(quarters[q], turn, 1) if turn else quarters[q]
            total = turned if total is None else jnp.where(lane // 32 == q, turned, total)
        strip.append(total)
    strip_e = strip[3]

    def strip_fields(values):
        high = [forward(value, False) for value in values]
        low = [{key: pltpu.roll(field[key], 16, 1) for key in field} for field in high]
        return pair_up(low, high)

    def next_slot(value):
        return pltpu.roll(value, width - 16, 1)

    fields = strip_fields(strip[:3])
    strip_high, strip_low = forces(fields, strip_e)
    s_strip = stresses(fields, strip_e)
    clamped = jnp.logical_and(gx == 0, lane < 32)
    strip_w = []
    for c in range(3):
        modes = {key: strip_high[c][key] + next_slot(strip_low[c][key]) for key in strip_high[c]}
        strip_w.append(jnp.where(clamped, 0.0, back(modes, False)))
    for r in range(6):
        ssb_ref[r] = spread(s_strip[r] + next_slot(s_strip[r]), False)

    at_cut = lane == (width - 1) * other

    def mend(value, strip_value, p):
        turn = (-(16 * (p + 2) + 8)) % width
        turned = pltpu.roll(strip_value, turn, 1) if turn else strip_value
        return jnp.where(at_cut, turned, value)

    z_share = jnp.where(last_row, 1.0, 0.5)
    yz_share = z_share * jnp.where(jnp.logical_and(last_lane, gy == n_gy - 1), 1.0, 0.5)
    share = [yz_share * 0.5] * planes
    share[planes - 1] = jnp.where(has_right, share[0], yz_share)

    def mend_w(p):
        for c in range(3):
            w_ref[p + 1, c] = mend(w_ref[p + 1, c], strip_w[c], p)

    def put_stress(ref, p, below, above, strip_ref):
        for r in range(6):
            value = spread(below[r] + above[r], True)
            ref[p, r] = mend(value, strip_ref[r], p) * share[p]

    s_w, w_modes = {}, {}
    sums = [zero] * 4

    def modes_of_w(p):
        w_modes[p] = [forward(w_ref[p + 1, c], True) for c in range(3)]

    def w_element(p):
        scale = er[...] if p >= planes else e_ref[p]
        fields = pair_up(w_modes[p - 1], w_modes[p])
        if p < planes:
            sums[3] = sums[3] + energy(fields, scale)
        s_w[p] = stresses(fields, scale)

    def add_sums(p):
        for c in range(3):
            b, w = b_ref[p, c], w_ref[p + 1, c]
            sums[0] = sums[0] + b * b
            sums[1] = sums[1] + b * w
            sums[2] = sums[2] + w * w

    fields = strip_fields(strip_w)
    s_strip = stresses(fields, strip_e)
    counted = jnp.logical_and(lax.rem(lane, 16) == 8, jnp.logical_and(lane >= 32, lane < 32 + 16 * planes))
    counted = jnp.logical_and(counted, gy == 1)
    strip_energy = jnp.where(counted, energy(fields, strip_e), 0.0)
    for r in range(6):
        ssw_ref[r] = spread(s_strip[r] + next_slot(s_strip[r]), False)

    for p in range(1, planes - 1):
        mend_w(p)
        add_sums(p)
        modes_of_w(p)
    for p in range(2, planes - 1):
        w_element(p)
    for p in range(1, planes - 1):
        put_stress(sb_ref, p, s_b[p], s_b[p + 1], ssb_ref)

    arrived([B_RIGHT], [B_LEFT, E_LEFT])
    do_element(0, b_modes(-1), m2[0])
    do_element(planes, m2[planes - 1], b_modes(planes))
    for p in (0, planes - 1):
        raw_w(p)
        mend_w(p)
        add_sums(p)
        modes_of_w(p)
    w_element(1)
    w_element(planes - 1)
    for c in range(3):
        w_ref[0, c] = back(lows[0][c], True)
        w_ref[planes + 1, c] = back(highs[planes][c], True)
    for p in (0, planes - 1):
        put_stress(sb_ref, p, s_b[p], s_b[p + 1], ssb_ref)
    for p in range(1, planes - 1):
        put_stress(sw_ref, p, s_w[p], s_w[p + 1], ssw_ref)

    arrived([P_RIGHT], [])
    for c in range(3):
        w_ref[0, c] = jnp.where(gx == 0, 0.0, pp[c] + w_ref[0, c])
    mend_w(-1)
    modes_of_w(-1)
    w_element(0)
    sums[3] = jnp.where(jnp.logical_and(first_lane, gy == 1), 0.0, sums[3]) + strip_energy

    row8 = lax.broadcasted_iota(jnp.int32, (8, width), 0)
    partial = jnp.zeros((8, width), jnp.float32)
    for k, total in enumerate(sums):
        partial = jnp.where(row8 == k, jnp.sum(total, axis=0, keepdims=True), partial)
    red[...] = partial

    def send_sum(k):
        pltpu.make_async_remote_copy(
            src_ref=red, dst_ref=slots.at[k - 1], send_sem=red_send, recv_sem=red_recv,
            device_id=member(k), device_id_type=MESH).start()

    each_member(send_sum)

    put_stress(sw_ref, 0, s_w[0], s_w[1], ssw_ref)
    arrived([], [Q_LEFT])
    for c in range(3):
        w_ref[planes + 1, c] = qq[c] + w_ref[planes + 1, c]
    mend_w(planes)
    modes_of_w(planes)
    w_element(planes)
    put_stress(sw_ref, planes - 1, s_w[planes - 1], s_w[planes], ssw_ref)

    pltpu.make_async_copy(slots, slots, red_recv).wait()
    total = red[...]
    if n <= 32:
        for k in range(n - 1):
            total = total + slots[k]
    else:
        total = lax.fori_loop(0, n - 1, lambda k, value: value + slots[k], total)
    whole = jnp.broadcast_to(jnp.sum(total, axis=1, keepdims=True), (8, width))
    bb, bw, ww, wkw = (whole[k : k + 1] for k in range(4))
    first_step = bb / bw
    norm = bb - 2.0 * first_step * bw + first_step * first_step * ww
    ratio = norm / bb
    grown = 1.0 + ratio
    curve = grown * grown * bw - 2.0 * grown * first_step * ww + first_step * first_step * wkw
    second_step = norm / curve
    on_b = first_step + second_step * grown
    on_w = -second_step * first_step
    for p in range(planes):
        for c in range(3):
            x_out[c, pl.ds(p, depth, stride=planes), :] = on_b * b_ref[p, c] + on_w * w_ref[p + 1, c]
        for r in range(6):
            s_out[r, pl.ds(p, depth, stride=planes), :] = on_b * sb_ref[p, r] + on_w * sw_ref[p, r]

    to_other.wait_send()
    pltpu.make_async_copy(slots, slots, red_send).wait()

    @pl.when(has_right)
    def _():
        for copy in to_right.values():
            copy.wait_send()

    @pl.when(has_left)
    def _():
        for copy in to_left.values():
            copy.wait_send()


def solution(mesh):
    n_gx, n_gy = mesh.shape["gx"], mesh.shape["gy"]

    def per_device(body_force, modulus):
        depth, planes, width = modulus.shape
        assert n_gy == 2 and planes == 4 and width == 128
        rows = depth * planes
        n = n_gx * n_gy
        plane = (depth, width)
        vmem = lambda *dims: pltpu.VMEM(dims, jnp.float32)
        field, stress = pl.pallas_call(
            functools.partial(kernel, n_gx, n_gy),
            out_shape=(
                jax.ShapeDtypeStruct((3, rows, width), jnp.float32),
                jax.ShapeDtypeStruct((6, rows, width), jnp.float32),
            ),
            in_specs=[pl.BlockSpec(memory_space=pltpu.HBM)] * 2,
            out_specs=(pl.BlockSpec(memory_space=pltpu.VMEM),) * 2,
            scratch_shapes=[
                vmem(3, rows, width),
                vmem(rows, width),
                vmem(planes, 3, *plane),
                vmem(planes, *plane),
                vmem(3, *plane),
                vmem(3, *plane),
                vmem(3, *plane),
                vmem(*plane),
                vmem(3, *plane),
                vmem(3, *plane),
                vmem(3, *plane),
                vmem(2, *plane),
                vmem(2, *plane),
                vmem(4, *plane),
                vmem(planes + 2, 3, *plane),
                vmem(planes, 6, *plane),
                vmem(planes, 6, *plane),
                vmem(6, *plane),
                vmem(6, *plane),
                vmem(8, width),
                vmem(n - 1, 8, width),
                pltpu.SemaphoreType.DMA((2,)),
                pltpu.SemaphoreType.DMA((10,)),
                pltpu.SemaphoreType.DMA((10,)),
                pltpu.SemaphoreType.DMA,
                pltpu.SemaphoreType.DMA,
            ],
            compiler_params=pltpu.CompilerParams(
                collective_id=0, has_side_effects=True, vmem_limit_bytes=32 * 1024 * 1024
            ),
        )(body_force.reshape(3, rows, width), modulus.reshape(rows, width))
        return (
            field.reshape(3, depth, planes, width),
            stress.reshape(6, depth, planes, width),
        )

    return jax.shard_map(
        per_device,
        mesh=mesh,
        in_specs=(P(None, "sample", "gx", "gy"), P("sample", "gx", "gy")),
        out_specs=(P(None, "sample", "gx", "gy"), P(None, "sample", "gx", "gy")),
        check_vma=False,
    )
```

```python
import functools
import math

import jax
import jax.numpy as jnp
import numpy as np
from jax import lax
from jax.experimental import pallas as pl
from jax.experimental.pallas import tpu as pltpu
from jax.sharding import PartitionSpec as P

MESH = pl.DeviceIdType.MESH


def corner_list():
    return [(off_z, off_x, off_y) for off_z in (0, 1) for off_x in (0, 1) for off_y in (0, 1)]


def strain_matrix(point):
    corners = corner_list()
    grads = np.zeros((3, 8))
    for corner, offsets in enumerate(corners):
        for axis in range(3):
            value = 1.0 if offsets[axis] else -1.0
            for other in range(3):
                if other != axis:
                    value = value * (point[other] if offsets[other] else 1.0 - point[other])
            grads[axis, corner] = value
    strain = np.zeros((6, 24))
    for corner in range(8):
        for axis in range(3):
            strain[axis, axis * 8 + corner] = grads[axis, corner]
        strain[3, 0 * 8 + corner] = grads[1, corner]
        strain[3, 1 * 8 + corner] = grads[0, corner]
        strain[4, 1 * 8 + corner] = grads[2, corner]
        strain[4, 2 * 8 + corner] = grads[1, corner]
        strain[5, 0 * 8 + corner] = grads[2, corner]
        strain[5, 2 * 8 + corner] = grads[0, corner]
    return strain


def modal_tables():
    poisson = 0.3
    lame_first = poisson / ((1.0 + poisson) * (1.0 - 2.0 * poisson))
    shear_mod = 1.0 / (2.0 * (1.0 + poisson))
    elastic = np.zeros((6, 6))
    elastic[:3, :3] = lame_first
    for axis in range(3):
        elastic[axis, axis] += 2.0 * shear_mod
        elastic[axis + 3, axis + 3] = shear_mod
    gauss_pts = [0.5 - 0.5 / math.sqrt(3.0), 0.5 + 0.5 / math.sqrt(3.0)]
    stiffness = np.zeros((24, 24))
    for first in gauss_pts:
        for second in gauss_pts:
            for third in gauss_pts:
                strain = strain_matrix((first, second, third))
                stiffness += strain.T @ elastic @ strain / 8.0
    stress_map = elastic @ strain_matrix((0.5, 0.5, 0.5))
    pair = np.array([[1.0, 1.0], [-1.0, 1.0]])
    modes = np.kron(np.eye(3), np.kron(pair, np.kron(pair, pair)))
    stiffness = modes @ stiffness @ modes.T / 64.0
    stress_map = stress_map @ modes.T / 8.0

    def rows_of(matrix):
        out = []
        for row in matrix:
            terms = [(q // 8, (q % 8) // 4, (q % 4) // 2, q % 2, float(v)) for q, v in enumerate(row) if abs(v) > 1e-9]
            out.append(terms)
        return out

    return rows_of(stiffness), rows_of(stress_map)


STIFF, STRESS = modal_tables()
B_RIGHT, P_RIGHT, S_RIGHT, D_RIGHT, B_LEFT, E_LEFT, Q_LEFT, S_LEFT, D_LEFT, S_OTHER = range(10)


def combine(terms, fields):
    total = None
    for c, a, b, d, value in terms:
        part = fields[c][a, b, d] * np.float32(value)
        total = part if total is None else total + part
    return total


def kernel(n_gx, n_gy, f_hbm, e_hbm, x_out, s_out,
           f_in, e_in, b_ref, e_ref, bl, pp, br, er, qq, p_out, q_out,
           msg, st_same, st_other, w_ref, sb_ref, sw_ref, ssb_ref, ssw_ref,
           red, slots, in_sem, send_sem, recv_sem, red_send, red_recv):
    gx, gy = lax.axis_index("gx"), lax.axis_index("gy")
    rows = e_hbm.shape[0]
    planes, depth, width = b_ref.shape[0], b_ref.shape[2], b_ref.shape[3]
    has_left, has_right = gx > 0, gx < n_gx - 1
    other = 1 - gy
    n = n_gx * n_gy
    me = gx * n_gy + gy

    load_f = pltpu.make_async_copy(f_hbm, f_in, in_sem.at[0])
    load_e = pltpu.make_async_copy(e_hbm, e_in, in_sem.at[1])
    load_f.start()
    load_e.start()

    barrier = pltpu.get_barrier_semaphore()

    def member(k):
        target = lax.rem(me + k, n)
        return {"gx": target // n_gy, "gy": lax.rem(target, n_gy)}

    def each_member(body):
        if n <= 32:
            for k in range(1, n):
                body(k)
        else:
            lax.fori_loop(1, n, lambda k, carry: (body(k), carry)[1], 0)

    each_member(lambda k: pl.semaphore_signal(barrier, inc=1, device_id=member(k), device_id_type=MESH))

    shape = (depth, width)
    lane = lax.broadcasted_iota(jnp.int32, shape, 1)
    row = lax.broadcasted_iota(jnp.int32, shape, 0)
    zero = jnp.zeros(shape, jnp.float32)
    first_row, last_row = row == 0, row == depth - 1
    first_lane, last_lane = lane == 0, lane == width - 1

    @pl.when(gx == 0)
    def _():
        bl[...] = jnp.zeros_like(bl)
        pp[...] = jnp.zeros_like(pp)
        st_same[0] = zero
        st_other[0] = zero

    @pl.when(gx == n_gx - 1)
    def _():
        br[...] = jnp.zeros_like(br)
        er[...] = jnp.zeros_like(er)
        qq[...] = jnp.zeros_like(qq)
        st_same[1] = zero
        st_other[3] = zero

    def remote(src, dst, which, x, y):
        return pltpu.make_async_remote_copy(
            src_ref=src, dst_ref=dst, send_sem=send_sem.at[which], recv_sem=recv_sem.at[which],
            device_id={"gx": x, "gy": y}, device_id_type=MESH)

    right, left = lax.rem(gx + 1, n_gx), lax.rem(gx + n_gx - 1, n_gx)
    to_right = {
        B_RIGHT: remote(b_ref.at[planes - 1], bl, B_RIGHT, right, gy),
        P_RIGHT: remote(p_out, pp, P_RIGHT, right, gy),
        S_RIGHT: remote(msg.at[1], st_same.at[0], S_RIGHT, right, gy),
        D_RIGHT: remote(msg.at[1], st_other.at[0], D_RIGHT, right, other),
    }
    to_left = {
        B_LEFT: remote(b_ref.at[0], br, B_LEFT, left, gy),
        E_LEFT: remote(e_ref.at[0], er, E_LEFT, left, gy),
        Q_LEFT: remote(q_out, qq, Q_LEFT, left, gy),
        S_LEFT: remote(msg.at[0], st_same.at[1], S_LEFT, left, gy),
        D_LEFT: remote(msg.at[0], st_other.at[3], D_LEFT, left, other),
    }
    to_other = remote(msg, st_other.at[pl.ds(1, 2)], S_OTHER, gx, other)

    def start(rights, lefts):
        @pl.when(has_right)
        def _():
            for which in rights:
                to_right[which].start()

        @pl.when(has_left)
        def _():
            for which in lefts:
                to_left[which].start()

    def arrived(rights, lefts):
        @pl.when(has_left)
        def _():
            for which in rights:
                to_right[which].wait_recv()

        @pl.when(has_right)
        def _():
            for which in lefts:
                to_left[which].wait_recv()

    def take(p):
        for c in range(3):
            b_ref[p, c] = f_in[c, pl.ds(p, depth, stride=planes), :]
        e_ref[p] = e_in[pl.ds(p, depth, stride=planes), :]

    load_f.wait()
    load_e.wait()
    take(planes - 1)
    take(0)
    pl.semaphore_wait(barrier, n - 1)
    start([B_RIGHT], [B_LEFT, E_LEFT])
    for p in range(1, planes - 1):
        take(p)

    for side in range(2):
        packed = None
        for c in range(4):
            for t in range(2):
                p = 2 * side + t
                value = b_ref[p, c] if c < 3 else e_ref[p]
                turned = pltpu.roll(value, (32 * c + 16 * t + 8) % width, 1)
                packed = turned if packed is None else jnp.where(lane // 16 == 2 * c + t, turned, packed)
        msg[side] = packed
    to_other.start()
    start([S_RIGHT, D_RIGHT], [S_LEFT, D_LEFT])

    def y_below(value, edge):
        value = pltpu.roll(value, 1, 1)
        return jnp.where(first_lane, 0.0, value) if edge else value

    def y_above(value, edge):
        value = pltpu.roll(value, width - 1, 1)
        return jnp.where(last_lane, 0.0, value) if edge else value

    def z_below(value):
        return jnp.where(first_row, 0.0, pltpu.roll(value, 1, 0))

    def z_above(value):
        return jnp.where(last_row, 0.0, pltpu.roll(value, depth - 1, 0))

    def forward(value, edge):
        below = y_below(value, edge)
        out = {}
        for d, part in ((0, value + below), (1, value - below)):
            low = z_below(part)
            out[0, d], out[1, d] = part + low, part - low
        return out

    def pair_up(low, high):
        fields = []
        for c in range(3):
            field = {}
            for key in high[c]:
                a, d = key
                field[a, 0, d] = high[c][key] + low[c][key]
                field[a, 1, d] = high[c][key] - low[c][key]
            fields.append(field)
        return fields

    def forces(fields, scale):
        highs, lows = [], []
        for c in range(3):
            high, low = {}, {}
            for a in range(2):
                for d in range(2):
                    diff = combine(STIFF[c * 8 + 4 * a + 2 + d], fields) * scale
                    terms = STIFF[c * 8 + 4 * a + d]
                    if terms:
                        same = combine(terms, fields) * scale
                        high[a, d], low[a, d] = same + diff, same - diff
                    else:
                        high[a, d], low[a, d] = diff, -diff
            highs.append(high)
            lows.append(low)
        return highs, lows

    def back(modes, edge):
        parts = []
        for d in range(2):
            parts.append(modes[0, d] + modes[1, d] + z_above(modes[0, d] - modes[1, d]))
        return parts[0] + parts[1] + y_above(parts[0] - parts[1], edge)

    def add(first, second):
        return {key: first[key] + second[key] for key in first}

    def energy(fields, scale):
        total = None
        for c in range(3):
            for k in range(1, 8):
                part = combine(STIFF[c * 8 + k], fields) * fields[c][k // 4, (k % 4) // 2, k % 2]
                total = part if total is None else total + part
        return total * scale

    def stresses(fields, scale):
        return [combine(STRESS[r], fields) * scale for r in range(6)]

    def spread(value, edge):
        value = value + z_above(value)
        return value + y_above(value, edge)

    def b_plane(p, c):
        return bl[c] if p < 0 else br[c] if p >= planes else b_ref[p, c]

    def b_modes(p):
        return [forward(b_plane(p, c), True) for c in range(3)]

    m2 = [b_modes(p) for p in range(planes)]
    highs, lows, s_b = {}, {}, {}

    def do_element(p, low, high):
        scale = er[...] if p >= planes else e_ref[p]
        fields = pair_up(low, high)
        highs[p], lows[p] = forces(fields, scale)
        s_b[p] = stresses(fields, scale)

    do_element(planes - 1, m2[planes - 2], m2[planes - 1])
    for c in range(3):
        p_out[c] = back(highs[planes - 1][c], True)
    do_element(1, m2[0], m2[1])
    for c in range(3):
        q_out[c] = back(lows[1][c], True)
    start([P_RIGHT], [Q_LEFT])
    for p in range(2, planes - 1):
        do_element(p, m2[p - 1], m2[p])

    def raw_w(p):
        for c in range(3):
            w_ref[p + 1, c] = back(add(highs[p][c], lows[p + 1][c]), True)

    for p in range(1, planes - 1):
        raw_w(p)

    to_other.wait_recv()
    arrived([S_RIGHT, D_RIGHT], [S_LEFT, D_LEFT])
    mine = lax.rem(lane, 16) // 8 == gy
    quarters = [
        jnp.where(mine, st_same[0], st_other[0]),
        jnp.where(mine, msg[0], st_other[1]),
        jnp.where(mine, msg[1], st_other[2]),
        jnp.where(mine, st_same[1], st_other[3]),
    ]
    strip = []
    for c in range(4):
        total = None
        for q in range(4):
            turn = (32 * (q - c)) % width
            turned = pltpu.roll(quarters[q], turn, 1) if turn else quarters[q]
            total = turned if total is None else jnp.where(lane // 32 == q, turned, total)
        strip.append(total)
    strip_e = strip[3]

    def strip_fields(values):
        high = [forward(value, False) for value in values]
        low = [{key: pltpu.roll(field[key], 16, 1) for key in field} for field in high]
        return pair_up(low, high)

    def next_slot(value):
        return pltpu.roll(value, width - 16, 1)

    fields = strip_fields(strip[:3])
    strip_high, strip_low = forces(fields, strip_e)
    s_strip = stresses(fields, strip_e)
    clamped = jnp.logical_and(gx == 0, lane < 32)
    strip_w = []
    for c in range(3):
        modes = {key: strip_high[c][key] + next_slot(strip_low[c][key]) for key in strip_high[c]}
        strip_w.append(jnp.where(clamped, 0.0, back(modes, False)))
    for r in range(6):
        ssb_ref[r] = spread(s_strip[r] + next_slot(s_strip[r]), False)

    at_cut = lane == (width - 1) * other

    def mend(value, strip_value, p):
        turn = (-(16 * (p + 2) + 8)) % width
        turned = pltpu.roll(strip_value, turn, 1) if turn else strip_value
        return jnp.where(at_cut, turned, value)

    z_share = jnp.where(last_row, 1.0, 0.5)
    yz_share = z_share * jnp.where(jnp.logical_and(last_lane, gy == n_gy - 1), 1.0, 0.5)
    share = [yz_share * 0.5] * planes
    share[planes - 1] = jnp.where(has_right, share[0], yz_share)

    def mend_w(p):
        for c in range(3):
            w_ref[p + 1, c] = mend(w_ref[p + 1, c], strip_w[c], p)

    def put_stress(ref, p, below, above, strip_ref):
        for r in range(6):
            value = spread(below[r] + above[r], True)
            ref[p, r] = mend(value, strip_ref[r], p) * share[p]

    s_w, w_modes = {}, {}
    sums = [zero] * 4

    def modes_of_w(p):
        w_modes[p] = [forward(w_ref[p + 1, c], True) for c in range(3)]

    def w_element(p):
        scale = er[...] if p >= planes else e_ref[p]
        fields = pair_up(w_modes[p - 1], w_modes[p])
        if p < planes:
            sums[3] = sums[3] + energy(fields, scale)
        s_w[p] = stresses(fields, scale)

    def add_sums(p):
        for c in range(3):
            b, w = b_ref[p, c], w_ref[p + 1, c]
            sums[0] = sums[0] + b * b
            sums[1] = sums[1] + b * w
            sums[2] = sums[2] + w * w

    fields = strip_fields(strip_w)
    s_strip = stresses(fields, strip_e)
    counted = jnp.logical_and(lax.rem(lane, 16) == 8, jnp.logical_and(lane >= 32, lane < 32 + 16 * planes))
    counted = jnp.logical_and(counted, gy == 1)
    strip_energy = jnp.where(counted, energy(fields, strip_e), 0.0)
    for r in range(6):
        ssw_ref[r] = spread(s_strip[r] + next_slot(s_strip[r]), False)

    for p in range(1, planes - 1):
        mend_w(p)
        add_sums(p)
        modes_of_w(p)
    for p in range(2, planes - 1):
        w_element(p)
    for p in range(1, planes - 1):
        put_stress(sb_ref, p, s_b[p], s_b[p + 1], ssb_ref)

    arrived([B_RIGHT], [B_LEFT, E_LEFT])
    do_element(0, b_modes(-1), m2[0])
    do_element(planes, m2[planes - 1], b_modes(planes))
    for p in (0, planes - 1):
        raw_w(p)
        mend_w(p)
        add_sums(p)
        modes_of_w(p)
    w_element(1)
    w_element(planes - 1)
    for c in range(3):
        w_ref[0, c] = back(lows[0][c], True)
        w_ref[planes + 1, c] = back(highs[planes][c], True)
    for p in (0, planes - 1):
        put_stress(sb_ref, p, s_b[p], s_b[p + 1], ssb_ref)
    for p in range(1, planes - 1):
        put_stress(sw_ref, p, s_w[p], s_w[p + 1], ssw_ref)

    arrived([P_RIGHT], [])
    for c in range(3):
        w_ref[0, c] = jnp.where(gx == 0, 0.0, pp[c] + w_ref[0, c])
    mend_w(-1)
    modes_of_w(-1)
    w_element(0)
    sums[3] = jnp.where(jnp.logical_and(first_lane, gy == 1), 0.0, sums[3]) + strip_energy

    row8 = lax.broadcasted_iota(jnp.int32, (8, width), 0)
    partial = jnp.zeros((8, width), jnp.float32)
    for k, total in enumerate(sums):
        partial = jnp.where(row8 == k, jnp.sum(total, axis=0, keepdims=True), partial)
    red[...] = partial

    def send_sum(k):
        pltpu.make_async_remote_copy(
            src_ref=red, dst_ref=slots.at[k - 1], send_sem=red_send, recv_sem=red_recv,
            device_id=member(k), device_id_type=MESH).start()

    each_member(send_sum)

    put_stress(sw_ref, 0, s_w[0], s_w[1], ssw_ref)
    arrived([], [Q_LEFT])
    for c in range(3):
        w_ref[planes + 1, c] = qq[c] + w_ref[planes + 1, c]
    mend_w(planes)
    modes_of_w(planes)
    w_element(planes)
    put_stress(sw_ref, planes - 1, s_w[planes - 1], s_w[planes], ssw_ref)

    pltpu.make_async_copy(slots, slots, red_recv).wait()
    total = red[...]
    if n <= 32:
        for k in range(n - 1):
            total = total + slots[k]
    else:
        total = lax.fori_loop(0, n - 1, lambda k, value: value + slots[k], total)
    whole = jnp.broadcast_to(jnp.sum(total, axis=1, keepdims=True), (8, width))
    bb, bw, ww, wkw = (whole[k : k + 1] for k in range(4))
    first_step = bb / bw
    norm = bb - 2.0 * first_step * bw + first_step * first_step * ww
    ratio = norm / bb
    grown = 1.0 + ratio
    curve = grown * grown * bw - 2.0 * grown * first_step * ww + first_step * first_step * wkw
    second_step = norm / curve
    on_b = first_step + second_step * grown
    on_w = -second_step * first_step
    for p in range(planes):
        for c in range(3):
            x_out[c, pl.ds(p, depth, stride=planes), :] = on_b * b_ref[p, c] + on_w * w_ref[p + 1, c]
        for r in range(6):
            s_out[r, pl.ds(p, depth, stride=planes), :] = on_b * sb_ref[p, r] + on_w * sw_ref[p, r]

    to_other.wait_send()
    pltpu.make_async_copy(slots, slots, red_send).wait()

    @pl.when(has_right)
    def _():
        for copy in to_right.values():
            copy.wait_send()

    @pl.when(has_left)
    def _():
        for copy in to_left.values():
            copy.wait_send()


def store(x_ref, s_ref, x_out, s_out, sem):
    copies = [
        pltpu.make_async_copy(x_ref, x_out, sem.at[0]),
        pltpu.make_async_copy(s_ref, s_out, sem.at[1]),
    ]
    for copy in copies:
        copy.start()
    for copy in copies:
        copy.wait()


def solution(mesh):
    n_gx, n_gy = mesh.shape["gx"], mesh.shape["gy"]

    def per_device(body_force, modulus):
        depth, planes, width = modulus.shape
        assert n_gy == 2 and planes == 4 and width == 128
        rows = depth * planes
        n = n_gx * n_gy
        plane = (depth, width)
        vmem = lambda *dims: pltpu.VMEM(dims, jnp.float32)
        field, stress = pl.pallas_call(
            functools.partial(kernel, n_gx, n_gy),
            out_shape=(
                jax.ShapeDtypeStruct((3, rows, width), jnp.float32),
                jax.ShapeDtypeStruct((6, rows, width), jnp.float32),
            ),
            in_specs=[pl.BlockSpec(memory_space=pltpu.HBM)] * 2,
            out_specs=(pl.BlockSpec(memory_space=pltpu.VMEM),) * 2,
            scratch_shapes=[
                vmem(3, rows, width),
                vmem(rows, width),
                vmem(planes, 3, *plane),
                vmem(planes, *plane),
                vmem(3, *plane),
                vmem(3, *plane),
                vmem(3, *plane),
                vmem(*plane),
                vmem(3, *plane),
                vmem(3, *plane),
                vmem(3, *plane),
                vmem(2, *plane),
                vmem(2, *plane),
                vmem(4, *plane),
                vmem(planes + 2, 3, *plane),
                vmem(planes, 6, *plane),
                vmem(planes, 6, *plane),
                vmem(6, *plane),
                vmem(6, *plane),
                vmem(8, width),
                vmem(n - 1, 8, width),
                pltpu.SemaphoreType.DMA((2,)),
                pltpu.SemaphoreType.DMA((10,)),
                pltpu.SemaphoreType.DMA((10,)),
                pltpu.SemaphoreType.DMA,
                pltpu.SemaphoreType.DMA,
            ],
            compiler_params=pltpu.CompilerParams(
                collective_id=0, has_side_effects=True, vmem_limit_bytes=32 * 1024 * 1024
            ),
        )(
            pltpu.with_memory_space_constraint(body_force.reshape(3, rows, width), pltpu.HBM),
            pltpu.with_memory_space_constraint(modulus.reshape(rows, width), pltpu.HBM),
        )
        field, stress = pl.pallas_call(
            store,
            out_shape=(
                jax.ShapeDtypeStruct((3, rows, width), jnp.float32),
                jax.ShapeDtypeStruct((6, rows, width), jnp.float32),
            ),
            in_specs=[pl.BlockSpec(memory_space=pl.ANY)] * 2,
            out_specs=(pl.BlockSpec(memory_space=pl.ANY),) * 2,
            scratch_shapes=[pltpu.SemaphoreType.DMA((2,))],
        )(field, stress)
        return (
            field.reshape(3, depth, planes, width),
            stress.reshape(6, depth, planes, width),
        )

    return jax.shard_map(
        per_device,
        mesh=mesh,
        in_specs=(P(None, "sample", "gx", "gy"), P("sample", "gx", "gy")),
        out_specs=(P(None, "sample", "gx", "gy"), P(None, "sample", "gx", "gy")),
        check_vma=False,
    )
```

```python
import functools
import math

import jax
import jax.numpy as jnp
import numpy as np
from jax import lax
from jax.experimental import pallas as pl
from jax.experimental.pallas import tpu as pltpu
from jax.sharding import PartitionSpec as P

MESH = pl.DeviceIdType.MESH


def corner_list():
    return [(off_z, off_x, off_y) for off_z in (0, 1) for off_x in (0, 1) for off_y in (0, 1)]


def strain_matrix(point):
    corners = corner_list()
    grads = np.zeros((3, 8))
    for corner, offsets in enumerate(corners):
        for axis in range(3):
            value = 1.0 if offsets[axis] else -1.0
            for other in range(3):
                if other != axis:
                    value = value * (point[other] if offsets[other] else 1.0 - point[other])
            grads[axis, corner] = value
    strain = np.zeros((6, 24))
    for corner in range(8):
        for axis in range(3):
            strain[axis, axis * 8 + corner] = grads[axis, corner]
        strain[3, 0 * 8 + corner] = grads[1, corner]
        strain[3, 1 * 8 + corner] = grads[0, corner]
        strain[4, 1 * 8 + corner] = grads[2, corner]
        strain[4, 2 * 8 + corner] = grads[1, corner]
        strain[5, 0 * 8 + corner] = grads[2, corner]
        strain[5, 2 * 8 + corner] = grads[0, corner]
    return strain


def modal_tables():
    poisson = 0.3
    lame_first = poisson / ((1.0 + poisson) * (1.0 - 2.0 * poisson))
    shear_mod = 1.0 / (2.0 * (1.0 + poisson))
    elastic = np.zeros((6, 6))
    elastic[:3, :3] = lame_first
    for axis in range(3):
        elastic[axis, axis] += 2.0 * shear_mod
        elastic[axis + 3, axis + 3] = shear_mod
    gauss_pts = [0.5 - 0.5 / math.sqrt(3.0), 0.5 + 0.5 / math.sqrt(3.0)]
    stiffness = np.zeros((24, 24))
    for first in gauss_pts:
        for second in gauss_pts:
            for third in gauss_pts:
                strain = strain_matrix((first, second, third))
                stiffness += strain.T @ elastic @ strain / 8.0
    stress_map = elastic @ strain_matrix((0.5, 0.5, 0.5))
    pair = np.array([[1.0, 1.0], [-1.0, 1.0]])
    modes = np.kron(np.eye(3), np.kron(pair, np.kron(pair, pair)))
    stiffness = modes @ stiffness @ modes.T / 64.0
    stress_map = stress_map @ modes.T / 8.0

    def rows_of(matrix):
        out = []
        for row in matrix:
            terms = [(q // 8, (q % 8) // 4, (q % 4) // 2, q % 2, float(v)) for q, v in enumerate(row) if abs(v) > 1e-9]
            out.append(terms)
        return out

    return rows_of(stiffness), rows_of(stress_map)


STIFF, STRESS = modal_tables()
B_RIGHT, P_RIGHT, S_RIGHT, D_RIGHT, B_LEFT, E_LEFT, Q_LEFT, S_LEFT, D_LEFT, S_OTHER = range(10)


def combine(terms, fields):
    total = None
    for c, a, b, d, value in terms:
        part = fields[c][a, b, d] * np.float32(value)
        total = part if total is None else total + part
    return total


def kernel(n_gx, n_gy, f_hbm, e_hbm, x_out, s_out,
           f_in, e_in, b_ref, e_ref, bl, pp, br, er, qq, p_out, q_out,
           msg, st_same, st_other, w_ref, sb_ref, sw_ref, ssb_ref, ssw_ref,
           red, slots, in_sem, send_sem, recv_sem, red_send, red_recv):
    gx, gy = lax.axis_index("gx"), lax.axis_index("gy")
    rows = e_hbm.shape[0]
    planes, depth, width = b_ref.shape[0], b_ref.shape[2], b_ref.shape[3]
    has_left, has_right = gx > 0, gx < n_gx - 1
    other = 1 - gy
    n = n_gx * n_gy
    me = gx * n_gy + gy

    load_f = pltpu.make_async_copy(f_hbm, f_in, in_sem.at[0])
    load_e = pltpu.make_async_copy(e_hbm, e_in, in_sem.at[1])
    load_f.start()
    load_e.start()

    barrier = pltpu.get_barrier_semaphore()

    def member(k):
        target = lax.rem(me + k, n)
        return {"gx": target // n_gy, "gy": lax.rem(target, n_gy)}

    def each_member(body):
        if n <= 32:
            for k in range(1, n):
                body(k)
        else:
            lax.fori_loop(1, n, lambda k, carry: (body(k), carry)[1], 0)

    each_member(lambda k: pl.semaphore_signal(barrier, inc=1, device_id=member(k), device_id_type=MESH))

    shape = (depth, width)
    lane = lax.broadcasted_iota(jnp.int32, shape, 1)
    row = lax.broadcasted_iota(jnp.int32, shape, 0)
    zero = jnp.zeros(shape, jnp.float32)
    first_row, last_row = row == 0, row == depth - 1
    first_lane, last_lane = lane == 0, lane == width - 1

    @pl.when(gx == 0)
    def _():
        bl[...] = jnp.zeros_like(bl)
        pp[...] = jnp.zeros_like(pp)
        st_same[0] = zero
        st_other[0] = zero

    @pl.when(gx == n_gx - 1)
    def _():
        br[...] = jnp.zeros_like(br)
        er[...] = jnp.zeros_like(er)
        qq[...] = jnp.zeros_like(qq)
        st_same[1] = zero
        st_other[3] = zero

    def remote(src, dst, which, x, y):
        return pltpu.make_async_remote_copy(
            src_ref=src, dst_ref=dst, send_sem=send_sem.at[which], recv_sem=recv_sem.at[which],
            device_id={"gx": x, "gy": y}, device_id_type=MESH)

    right, left = lax.rem(gx + 1, n_gx), lax.rem(gx + n_gx - 1, n_gx)
    to_right = {
        B_RIGHT: remote(b_ref.at[planes - 1], bl, B_RIGHT, right, gy),
        P_RIGHT: remote(p_out, pp, P_RIGHT, right, gy),
        S_RIGHT: remote(msg.at[1], st_same.at[0], S_RIGHT, right, gy),
        D_RIGHT: remote(msg.at[1], st_other.at[0], D_RIGHT, right, other),
    }
    to_left = {
        B_LEFT: remote(b_ref.at[0], br, B_LEFT, left, gy),
        E_LEFT: remote(e_ref.at[0], er, E_LEFT, left, gy),
        Q_LEFT: remote(q_out, qq, Q_LEFT, left, gy),
        S_LEFT: remote(msg.at[0], st_same.at[1], S_LEFT, left, gy),
        D_LEFT: remote(msg.at[0], st_other.at[3], D_LEFT, left, other),
    }
    to_other = remote(msg, st_other.at[pl.ds(1, 2)], S_OTHER, gx, other)

    def start(rights, lefts):
        @pl.when(has_right)
        def _():
            for which in rights:
                to_right[which].start()

        @pl.when(has_left)
        def _():
            for which in lefts:
                to_left[which].start()

    def arrived(rights, lefts):
        @pl.when(has_left)
        def _():
            for which in rights:
                to_right[which].wait_recv()

        @pl.when(has_right)
        def _():
            for which in lefts:
                to_left[which].wait_recv()

    def take(p):
        for c in range(3):
            b_ref[p, c] = f_in[c, pl.ds(p, depth, stride=planes), :]
        e_ref[p] = e_in[pl.ds(p, depth, stride=planes), :]

    load_f.wait()
    load_e.wait()
    take(planes - 1)
    take(0)
    pl.semaphore_wait(barrier, n - 1)
    start([B_RIGHT], [B_LEFT, E_LEFT])
    for p in range(1, planes - 1):
        take(p)

    for side in range(2):
        packed = None
        for c in range(4):
            for t in range(2):
                p = 2 * side + t
                value = b_ref[p, c] if c < 3 else e_ref[p]
                turned = pltpu.roll(value, (32 * c + 16 * t + 8) % width, 1)
                packed = turned if packed is None else jnp.where(lane // 16 == 2 * c + t, turned, packed)
        msg[side] = packed
    to_other.start()
    start([S_RIGHT, D_RIGHT], [S_LEFT, D_LEFT])

    def y_below(value, edge):
        value = pltpu.roll(value, 1, 1)
        return jnp.where(first_lane, 0.0, value) if edge else value

    def y_above(value, edge):
        value = pltpu.roll(value, width - 1, 1)
        return jnp.where(last_lane, 0.0, value) if edge else value

    def z_below(value):
        return jnp.where(first_row, 0.0, pltpu.roll(value, 1, 0))

    def z_above(value):
        return jnp.where(last_row, 0.0, pltpu.roll(value, depth - 1, 0))

    def forward(value, edge):
        below = y_below(value, edge)
        out = {}
        for d, part in ((0, value + below), (1, value - below)):
            low = z_below(part)
            out[0, d], out[1, d] = part + low, part - low
        return out

    def pair_up(low, high):
        fields = []
        for c in range(3):
            field = {}
            for key in high[c]:
                a, d = key
                field[a, 0, d] = high[c][key] + low[c][key]
                field[a, 1, d] = high[c][key] - low[c][key]
            fields.append(field)
        return fields

    def forces(fields, scale):
        highs, lows = [], []
        for c in range(3):
            high, low = {}, {}
            for a in range(2):
                for d in range(2):
                    diff = combine(STIFF[c * 8 + 4 * a + 2 + d], fields) * scale
                    terms = STIFF[c * 8 + 4 * a + d]
                    if terms:
                        same = combine(terms, fields) * scale
                        high[a, d], low[a, d] = same + diff, same - diff
                    else:
                        high[a, d], low[a, d] = diff, -diff
            highs.append(high)
            lows.append(low)
        return highs, lows

    def back(modes, edge):
        parts = []
        for d in range(2):
            parts.append(modes[0, d] + modes[1, d] + z_above(modes[0, d] - modes[1, d]))
        return parts[0] + parts[1] + y_above(parts[0] - parts[1], edge)

    def add(first, second):
        return {key: first[key] + second[key] for key in first}

    def energy(fields, scale):
        total = None
        for c in range(3):
            for k in range(1, 8):
                part = combine(STIFF[c * 8 + k], fields) * fields[c][k // 4, (k % 4) // 2, k % 2]
                total = part if total is None else total + part
        return total * scale

    def stresses(fields, scale):
        return [combine(STRESS[r], fields) * scale for r in range(6)]

    def spread(value, edge):
        value = value + z_above(value)
        return value + y_above(value, edge)

    def b_plane(p, c):
        return bl[c] if p < 0 else br[c] if p >= planes else b_ref[p, c]

    def b_modes(p):
        return [forward(b_plane(p, c), True) for c in range(3)]

    m2 = [b_modes(p) for p in range(planes)]
    highs, lows, s_b = {}, {}, {}

    def do_element(p, low, high):
        scale = er[...] if p >= planes else e_ref[p]
        fields = pair_up(low, high)
        highs[p], lows[p] = forces(fields, scale)
        s_b[p] = stresses(fields, scale)

    do_element(planes - 1, m2[planes - 2], m2[planes - 1])
    for c in range(3):
        p_out[c] = back(highs[planes - 1][c], True)
    do_element(1, m2[0], m2[1])
    for c in range(3):
        q_out[c] = back(lows[1][c], True)
    start([P_RIGHT], [Q_LEFT])
    for p in range(2, planes - 1):
        do_element(p, m2[p - 1], m2[p])

    def raw_w(p):
        for c in range(3):
            w_ref[p + 1, c] = back(add(highs[p][c], lows[p + 1][c]), True)

    for p in range(1, planes - 1):
        raw_w(p)

    to_other.wait_recv()
    arrived([S_RIGHT, D_RIGHT], [S_LEFT, D_LEFT])
    mine = lax.rem(lane, 16) // 8 == gy
    quarters = [
        jnp.where(mine, st_same[0], st_other[0]),
        jnp.where(mine, msg[0], st_other[1]),
        jnp.where(mine, msg[1], st_other[2]),
        jnp.where(mine, st_same[1], st_other[3]),
    ]
    strip = []
    for c in range(4):
        total = None
        for q in range(4):
            turn = (32 * (q - c)) % width
            turned = pltpu.roll(quarters[q], turn, 1) if turn else quarters[q]
            total = turned if total is None else jnp.where(lane // 32 == q, turned, total)
        strip.append(total)
    strip_e = strip[3]

    def strip_fields(values):
        high = [forward(value, False) for value in values]
        low = [{key: pltpu.roll(field[key], 16, 1) for key in field} for field in high]
        return pair_up(low, high)

    def next_slot(value):
        return pltpu.roll(value, width - 16, 1)

    fields = strip_fields(strip[:3])
    strip_high, strip_low = forces(fields, strip_e)
    s_strip = stresses(fields, strip_e)
    clamped = jnp.logical_and(gx == 0, lane < 32)
    strip_w = []
    for c in range(3):
        modes = {key: strip_high[c][key] + next_slot(strip_low[c][key]) for key in strip_high[c]}
        strip_w.append(jnp.where(clamped, 0.0, back(modes, False)))
    for r in range(6):
        ssb_ref[r] = spread(s_strip[r] + next_slot(s_strip[r]), False)

    at_cut = lane == (width - 1) * other

    def mend(value, strip_value, p):
        turn = (-(16 * (p + 2) + 8)) % width
        turned = pltpu.roll(strip_value, turn, 1) if turn else strip_value
        return jnp.where(at_cut, turned, value)

    z_share = jnp.where(last_row, 1.0, 0.5)
    yz_share = z_share * jnp.where(jnp.logical_and(last_lane, gy == n_gy - 1), 1.0, 0.5)
    share = [yz_share * 0.5] * planes
    share[planes - 1] = jnp.where(has_right, share[0], yz_share)

    def mend_w(p):
        for c in range(3):
            w_ref[p + 1, c] = mend(w_ref[p + 1, c], strip_w[c], p)

    def put_stress(ref, p, below, above, strip_ref):
        for r in range(6):
            value = spread(below[r] + above[r], True)
            ref[p, r] = mend(value, strip_ref[r], p) * share[p]

    s_w, w_modes = {}, {}
    sums = [zero] * 4

    def modes_of_w(p):
        w_modes[p] = [forward(w_ref[p + 1, c], True) for c in range(3)]

    def w_element(p):
        scale = er[...] if p >= planes else e_ref[p]
        fields = pair_up(w_modes[p - 1], w_modes[p])
        if p < planes:
            sums[3] = sums[3] + energy(fields, scale)
        s_w[p] = stresses(fields, scale)

    def add_sums(p):
        for c in range(3):
            b, w = b_ref[p, c], w_ref[p + 1, c]
            sums[0] = sums[0] + b * b
            sums[1] = sums[1] + b * w
            sums[2] = sums[2] + w * w

    fields = strip_fields(strip_w)
    s_strip = stresses(fields, strip_e)
    counted = jnp.logical_and(lax.rem(lane, 16) == 8, jnp.logical_and(lane >= 32, lane < 32 + 16 * planes))
    counted = jnp.logical_and(counted, gy == 1)
    strip_energy = jnp.where(counted, energy(fields, strip_e), 0.0)
    for r in range(6):
        ssw_ref[r] = spread(s_strip[r] + next_slot(s_strip[r]), False)

    for p in range(1, planes - 1):
        mend_w(p)
        add_sums(p)
        modes_of_w(p)
    for p in range(2, planes - 1):
        w_element(p)
    for p in range(1, planes - 1):
        put_stress(sb_ref, p, s_b[p], s_b[p + 1], ssb_ref)

    arrived([B_RIGHT], [B_LEFT, E_LEFT])
    do_element(0, b_modes(-1), m2[0])
    do_element(planes, m2[planes - 1], b_modes(planes))
    for p in (0, planes - 1):
        raw_w(p)
        mend_w(p)
        add_sums(p)
        modes_of_w(p)
    w_element(1)
    w_element(planes - 1)
    for c in range(3):
        w_ref[0, c] = back(lows[0][c], True)
        w_ref[planes + 1, c] = back(highs[planes][c], True)
    for p in (0, planes - 1):
        put_stress(sb_ref, p, s_b[p], s_b[p + 1], ssb_ref)
    for p in range(1, planes - 1):
        put_stress(sw_ref, p, s_w[p], s_w[p + 1], ssw_ref)

    arrived([P_RIGHT], [])
    for c in range(3):
        w_ref[0, c] = jnp.where(gx == 0, 0.0, pp[c] + w_ref[0, c])
    mend_w(-1)
    modes_of_w(-1)
    w_element(0)
    sums[3] = jnp.where(jnp.logical_and(first_lane, gy == 1), 0.0, sums[3]) + strip_energy

    row8 = lax.broadcasted_iota(jnp.int32, (8, width), 0)
    partial = jnp.zeros((8, width), jnp.float32)
    for k, total in enumerate(sums):
        partial = jnp.where(row8 == k, jnp.sum(total, axis=0, keepdims=True), partial)
    red[...] = partial

    def send_sum(k):
        pltpu.make_async_remote_copy(
            src_ref=red, dst_ref=slots.at[k - 1], send_sem=red_send, recv_sem=red_recv,
            device_id=member(k), device_id_type=MESH).start()

    each_member(send_sum)

    put_stress(sw_ref, 0, s_w[0], s_w[1], ssw_ref)
    arrived([], [Q_LEFT])
    for c in range(3):
        w_ref[planes + 1, c] = qq[c] + w_ref[planes + 1, c]
    mend_w(planes)
    modes_of_w(planes)
    w_element(planes)
    put_stress(sw_ref, planes - 1, s_w[planes - 1], s_w[planes], ssw_ref)

    pltpu.make_async_copy(slots, slots, red_recv).wait()
    total = red[...]
    if n <= 32:
        for k in range(n - 1):
            total = total + slots[k]
    else:
        total = lax.fori_loop(0, n - 1, lambda k, value: value + slots[k], total)
    whole = jnp.broadcast_to(jnp.sum(total, axis=1, keepdims=True), (8, width))
    bb, bw, ww, wkw = (whole[k : k + 1] for k in range(4))
    first_step = bb / bw
    norm = bb - 2.0 * first_step * bw + first_step * first_step * ww
    ratio = norm / bb
    grown = 1.0 + ratio
    curve = grown * grown * bw - 2.0 * grown * first_step * ww + first_step * first_step * wkw
    second_step = norm / curve
    on_b = first_step + second_step * grown
    on_w = -second_step * first_step
    for p in range(planes):
        for c in range(3):
            x_out[c, pl.ds(p, depth, stride=planes), :] = on_b * b_ref[p, c] + on_w * w_ref[p + 1, c]
        for r in range(6):
            s_out[r, pl.ds(p, depth, stride=planes), :] = on_b * sb_ref[p, r] + on_w * sw_ref[p, r]

    to_other.wait_send()
    pltpu.make_async_copy(slots, slots, red_send).wait()

    @pl.when(has_right)
    def _():
        for copy in to_right.values():
            copy.wait_send()

    @pl.when(has_left)
    def _():
        for copy in to_left.values():
            copy.wait_send()


def solution(mesh):
    n_gx, n_gy = mesh.shape["gx"], mesh.shape["gy"]

    def per_device(body_force, modulus):
        depth, planes, width = modulus.shape
        assert n_gy == 2 and planes == 4 and width == 128
        rows = depth * planes
        n = n_gx * n_gy
        plane = (depth, width)
        vmem = lambda *dims: pltpu.VMEM(dims, jnp.float32)
        field, stress = pl.pallas_call(
            functools.partial(kernel, n_gx, n_gy),
            out_shape=(
                jax.ShapeDtypeStruct((3, rows, width), jnp.float32),
                jax.ShapeDtypeStruct((6, rows, width), jnp.float32),
            ),
            in_specs=[pl.BlockSpec(memory_space=pltpu.HBM)] * 2,
            out_specs=(pl.BlockSpec(memory_space=pltpu.VMEM),) * 2,
            scratch_shapes=[
                vmem(3, rows, width),
                vmem(rows, width),
                vmem(planes, 3, *plane),
                vmem(planes, *plane),
                vmem(3, *plane),
                vmem(3, *plane),
                vmem(3, *plane),
                vmem(*plane),
                vmem(3, *plane),
                vmem(3, *plane),
                vmem(3, *plane),
                vmem(2, *plane),
                vmem(2, *plane),
                vmem(4, *plane),
                vmem(planes + 2, 3, *plane),
                vmem(planes, 6, *plane),
                vmem(planes, 6, *plane),
                vmem(6, *plane),
                vmem(6, *plane),
                vmem(8, width),
                vmem(n - 1, 8, width),
                pltpu.SemaphoreType.DMA((2,)),
                pltpu.SemaphoreType.DMA((10,)),
                pltpu.SemaphoreType.DMA((10,)),
                pltpu.SemaphoreType.DMA,
                pltpu.SemaphoreType.DMA,
            ],
            compiler_params=pltpu.CompilerParams(
                collective_id=0, has_side_effects=True, vmem_limit_bytes=32 * 1024 * 1024
            ),
        )(
            pltpu.with_memory_space_constraint(body_force.reshape(3, rows, width), pltpu.HBM),
            pltpu.with_memory_space_constraint(modulus.reshape(rows, width), pltpu.HBM),
        )
        return (
            field.reshape(3, depth, planes, width),
            stress.reshape(6, depth, planes, width),
        )

    return jax.shard_map(
        per_device,
        mesh=mesh,
        in_specs=(P(None, "sample", "gx", "gy"), P("sample", "gx", "gy")),
        out_specs=(P(None, "sample", "gx", "gy"), P(None, "sample", "gx", "gy")),
        check_vma=False,
    )
```

```python
import functools
import math

import jax
import jax.numpy as jnp
import numpy as np
from jax import lax
from jax.experimental import pallas as pl
from jax.experimental.pallas import tpu as pltpu
from jax.sharding import PartitionSpec as P

MESH = pl.DeviceIdType.MESH


def corner_list():
    return [(off_z, off_x, off_y) for off_z in (0, 1) for off_x in (0, 1) for off_y in (0, 1)]


def strain_matrix(point):
    corners = corner_list()
    grads = np.zeros((3, 8))
    for corner, offsets in enumerate(corners):
        for axis in range(3):
            value = 1.0 if offsets[axis] else -1.0
            for other in range(3):
                if other != axis:
                    value = value * (point[other] if offsets[other] else 1.0 - point[other])
            grads[axis, corner] = value
    strain = np.zeros((6, 24))
    for corner in range(8):
        for axis in range(3):
            strain[axis, axis * 8 + corner] = grads[axis, corner]
        strain[3, 0 * 8 + corner] = grads[1, corner]
        strain[3, 1 * 8 + corner] = grads[0, corner]
        strain[4, 1 * 8 + corner] = grads[2, corner]
        strain[4, 2 * 8 + corner] = grads[1, corner]
        strain[5, 0 * 8 + corner] = grads[2, corner]
        strain[5, 2 * 8 + corner] = grads[0, corner]
    return strain


def modal_tables():
    poisson = 0.3
    lame_first = poisson / ((1.0 + poisson) * (1.0 - 2.0 * poisson))
    shear_mod = 1.0 / (2.0 * (1.0 + poisson))
    elastic = np.zeros((6, 6))
    elastic[:3, :3] = lame_first
    for axis in range(3):
        elastic[axis, axis] += 2.0 * shear_mod
        elastic[axis + 3, axis + 3] = shear_mod
    gauss_pts = [0.5 - 0.5 / math.sqrt(3.0), 0.5 + 0.5 / math.sqrt(3.0)]
    stiffness = np.zeros((24, 24))
    for first in gauss_pts:
        for second in gauss_pts:
            for third in gauss_pts:
                strain = strain_matrix((first, second, third))
                stiffness += strain.T @ elastic @ strain / 8.0
    stress_map = elastic @ strain_matrix((0.5, 0.5, 0.5))
    pair = np.array([[1.0, 1.0], [-1.0, 1.0]])
    modes = np.kron(np.eye(3), np.kron(pair, np.kron(pair, pair)))
    stiffness = modes @ stiffness @ modes.T / 64.0
    stress_map = stress_map @ modes.T / 8.0

    def rows_of(matrix):
        out = []
        for row in matrix:
            terms = [(q // 8, (q % 8) // 4, (q % 4) // 2, q % 2, float(v)) for q, v in enumerate(row) if abs(v) > 1e-9]
            out.append(terms)
        return out

    return rows_of(stiffness), rows_of(stress_map)


STIFF, STRESS = modal_tables()
B_RIGHT, P_RIGHT, S_RIGHT, D_RIGHT, B_LEFT, E_LEFT, Q_LEFT, S_LEFT, D_LEFT, S_OTHER = range(10)


def combine(terms, fields):
    total = None
    for c, a, b, d, value in terms:
        part = fields[c][a, b, d] * np.float32(value)
        total = part if total is None else total + part
    return total


def kernel(n_gx, n_gy, f_hbm, e_hbm, x_out, s_out,
           f_in, e_in, b_ref, e_ref, bl, pp, br, er, qq, p_out, q_out,
           msg, st_same, st_other, w_ref, bm_ref, wm_ref, high_ref, low_ref, sbe_ref, swe_ref, sb_ref, sw_ref, ssb_ref, ssw_ref,
           red, slots, in_sem, send_sem, recv_sem, red_send, red_recv):
    gx, gy = lax.axis_index("gx"), lax.axis_index("gy")
    rows = e_hbm.shape[0]
    planes, depth, width = b_ref.shape[0], b_ref.shape[2], b_ref.shape[3]
    has_left, has_right = gx > 0, gx < n_gx - 1
    other = 1 - gy
    n = n_gx * n_gy
    me = gx * n_gy + gy

    load_f = pltpu.make_async_copy(f_hbm, f_in, in_sem.at[0])
    load_e = pltpu.make_async_copy(e_hbm, e_in, in_sem.at[1])
    load_f.start()
    load_e.start()

    barrier = pltpu.get_barrier_semaphore()

    def member(k):
        target = lax.rem(me + k, n)
        return {"gx": target // n_gy, "gy": lax.rem(target, n_gy)}

    def each_member(body):
        if n <= 32:
            for k in range(1, n):
                body(k)
        else:
            lax.fori_loop(1, n, lambda k, carry: (body(k), carry)[1], 0)

    each_member(lambda k: pl.semaphore_signal(barrier, inc=1, device_id=member(k), device_id_type=MESH))

    shape = (depth, width)
    lane = lax.broadcasted_iota(jnp.int32, shape, 1)
    row = lax.broadcasted_iota(jnp.int32, shape, 0)
    zero = jnp.zeros(shape, jnp.float32)
    first_row, last_row = row == 0, row == depth - 1
    first_lane, last_lane = lane == 0, lane == width - 1

    @pl.when(gx == 0)
    def _():
        bl[...] = jnp.zeros_like(bl)
        pp[...] = jnp.zeros_like(pp)
        st_same[0] = zero
        st_other[0] = zero

    @pl.when(gx == n_gx - 1)
    def _():
        br[...] = jnp.zeros_like(br)
        er[...] = jnp.zeros_like(er)
        qq[...] = jnp.zeros_like(qq)
        st_same[1] = zero
        st_other[3] = zero

    def remote(src, dst, which, x, y):
        return pltpu.make_async_remote_copy(
            src_ref=src, dst_ref=dst, send_sem=send_sem.at[which], recv_sem=recv_sem.at[which],
            device_id={"gx": x, "gy": y}, device_id_type=MESH)

    right, left = lax.rem(gx + 1, n_gx), lax.rem(gx + n_gx - 1, n_gx)
    to_right = {
        B_RIGHT: remote(b_ref.at[planes - 1], bl, B_RIGHT, right, gy),
        P_RIGHT: remote(p_out, pp, P_RIGHT, right, gy),
        S_RIGHT: remote(msg.at[1], st_same.at[0], S_RIGHT, right, gy),
        D_RIGHT: remote(msg.at[1], st_other.at[0], D_RIGHT, right, other),
    }
    to_left = {
        B_LEFT: remote(b_ref.at[0], br, B_LEFT, left, gy),
        E_LEFT: remote(e_ref.at[0], er, E_LEFT, left, gy),
        Q_LEFT: remote(q_out, qq, Q_LEFT, left, gy),
        S_LEFT: remote(msg.at[0], st_same.at[1], S_LEFT, left, gy),
        D_LEFT: remote(msg.at[0], st_other.at[3], D_LEFT, left, other),
    }
    to_other = remote(msg, st_other.at[pl.ds(1, 2)], S_OTHER, gx, other)

    def start(rights, lefts):
        @pl.when(has_right)
        def _():
            for which in rights:
                to_right[which].start()

        @pl.when(has_left)
        def _():
            for which in lefts:
                to_left[which].start()

    def arrived(rights, lefts):
        @pl.when(has_left)
        def _():
            for which in rights:
                to_right[which].wait_recv()

        @pl.when(has_right)
        def _():
            for which in lefts:
                to_left[which].wait_recv()

    def take(p):
        for c in range(3):
            b_ref[p, c] = f_in[c, pl.ds(p, depth, stride=planes), :]
        e_ref[p] = e_in[pl.ds(p, depth, stride=planes), :]

    load_f.wait()
    load_e.wait()
    take(planes - 1)
    take(0)
    pl.semaphore_wait(barrier, n - 1)
    start([B_RIGHT], [B_LEFT, E_LEFT])
    for p in range(1, planes - 1):
        take(p)

    for side in range(2):
        packed = None
        for c in range(4):
            for t in range(2):
                p = 2 * side + t
                value = b_ref[p, c] if c < 3 else e_ref[p]
                turned = pltpu.roll(value, (32 * c + 16 * t + 8) % width, 1)
                packed = turned if packed is None else jnp.where(lane // 16 == 2 * c + t, turned, packed)
        msg[side] = packed
    to_other.start()
    start([S_RIGHT, D_RIGHT], [S_LEFT, D_LEFT])

    def y_below(value, edge):
        value = pltpu.roll(value, 1, 1)
        return jnp.where(first_lane, 0.0, value) if edge else value

    def y_above(value, edge):
        value = pltpu.roll(value, width - 1, 1)
        return jnp.where(last_lane, 0.0, value) if edge else value

    def z_below(value):
        return jnp.where(first_row, 0.0, pltpu.roll(value, 1, 0))

    def z_above(value):
        return jnp.where(last_row, 0.0, pltpu.roll(value, depth - 1, 0))

    def forward(value, edge):
        below = y_below(value, edge)
        out = {}
        for d, part in ((0, value + below), (1, value - below)):
            low = z_below(part)
            out[0, d], out[1, d] = part + low, part - low
        return out

    def pair_up(low, high):
        fields = []
        for c in range(3):
            field = {}
            for key in high[c]:
                a, d = key
                field[a, 0, d] = high[c][key] + low[c][key]
                field[a, 1, d] = high[c][key] - low[c][key]
            fields.append(field)
        return fields

    def forces(fields, scale):
        highs, lows = [], []
        for c in range(3):
            high, low = {}, {}
            for a in range(2):
                for d in range(2):
                    diff = combine(STIFF[c * 8 + 4 * a + 2 + d], fields) * scale
                    terms = STIFF[c * 8 + 4 * a + d]
                    if terms:
                        same = combine(terms, fields) * scale
                        high[a, d], low[a, d] = same + diff, same - diff
                    else:
                        high[a, d], low[a, d] = diff, -diff
            highs.append(high)
            lows.append(low)
        return highs, lows

    def back(modes, edge):
        parts = []
        for d in range(2):
            parts.append(modes[0, d] + modes[1, d] + z_above(modes[0, d] - modes[1, d]))
        return parts[0] + parts[1] + y_above(parts[0] - parts[1], edge)

    def add(first, second):
        return {key: first[key] + second[key] for key in first}

    def energy(fields, scale):
        total = None
        for c in range(3):
            for k in range(1, 8):
                part = combine(STIFF[c * 8 + k], fields) * fields[c][k // 4, (k % 4) // 2, k % 2]
                total = part if total is None else total + part
        return total * scale

    def stresses(fields, scale):
        return [combine(STRESS[r], fields) * scale for r in range(6)]

    def spread(value, edge):
        value = value + z_above(value)
        return value + y_above(value, edge)

    def b_plane(p, c):
        return bl[c] if p < 0 else br[c] if p >= planes else b_ref[p, c]

    def keep_modes(ref, p, values):
        for c in range(3):
            for (a, d), value in forward(values[c], True).items():
                ref[p + 1, 4 * c + 2 * a + d] = value

    def keep_b_modes(p):
        keep_modes(bm_ref, p, [b_plane(p, c) for c in range(3)])

    def tile_fields(ref, p, tile):
        def side(k):
            return [{(a, d): ref[k, 4 * c + 2 * a + d, tile, :] for a in range(2) for d in range(2)} for c in range(3)]
        return pair_up(side(p), side(p + 1))

    def tile_scale(p, tile):
        return er[tile, :] if p >= planes else e_ref[p, tile, :]

    def tiles(body, carry):
        return lax.fori_loop(0, depth // 8, lambda t, value: body(pl.ds(pl.multiple_of(8 * t, 8), 8), value), carry)

    def keep_stress(ref, p, tile, fields, scale):
        for r, value in enumerate(stresses(fields, scale)):
            ref[p, r, tile, :] = value

    def do_element(p):
        def body(tile, carry):
            fields, scale = tile_fields(bm_ref, p, tile), tile_scale(p, tile)
            high, low = forces(fields, scale)
            for c in range(3):
                for a, d in high[c]:
                    high_ref[p, 4 * c + 2 * a + d, tile, :] = high[c][a, d]
                    low_ref[p, 4 * c + 2 * a + d, tile, :] = low[c][a, d]
            keep_stress(sbe_ref, p, tile, fields, scale)
            return carry

        tiles(body, 0)

    def kept(ref, p, c):
        return {(a, d): ref[p, 4 * c + 2 * a + d] for a in range(2) for d in range(2)}

    keep_b_modes(planes - 2)
    keep_b_modes(planes - 1)
    do_element(planes - 1)
    for c in range(3):
        p_out[c] = back(kept(high_ref, planes - 1, c), True)
    keep_b_modes(0)
    keep_b_modes(1)
    do_element(1)
    for c in range(3):
        q_out[c] = back(kept(low_ref, 1, c), True)
    start([P_RIGHT], [Q_LEFT])
    for p in range(2, planes - 1):
        do_element(p)

    def raw_w(p):
        for c in range(3):
            w_ref[p + 1, c] = back(add(kept(high_ref, p, c), kept(low_ref, p + 1, c)), True)

    for p in range(1, planes - 1):
        raw_w(p)

    to_other.wait_recv()
    arrived([S_RIGHT, D_RIGHT], [S_LEFT, D_LEFT])
    mine = lax.rem(lane, 16) // 8 == gy
    quarters = [
        jnp.where(mine, st_same[0], st_other[0]),
        jnp.where(mine, msg[0], st_other[1]),
        jnp.where(mine, msg[1], st_other[2]),
        jnp.where(mine, st_same[1], st_other[3]),
    ]
    strip = []
    for c in range(4):
        total = None
        for q in range(4):
            turn = (32 * (q - c)) % width
            turned = pltpu.roll(quarters[q], turn, 1) if turn else quarters[q]
            total = turned if total is None else jnp.where(lane // 32 == q, turned, total)
        strip.append(total)
    strip_e = strip[3]

    def strip_fields(values):
        high = [forward(value, False) for value in values]
        low = [{key: pltpu.roll(field[key], 16, 1) for key in field} for field in high]
        return pair_up(low, high)

    def next_slot(value):
        return pltpu.roll(value, width - 16, 1)

    fields = strip_fields(strip[:3])
    strip_high, strip_low = forces(fields, strip_e)
    s_strip = stresses(fields, strip_e)
    clamped = jnp.logical_and(gx == 0, lane < 32)
    strip_w = []
    for c in range(3):
        modes = {key: strip_high[c][key] + next_slot(strip_low[c][key]) for key in strip_high[c]}
        strip_w.append(jnp.where(clamped, 0.0, back(modes, False)))
    for r in range(6):
        ssb_ref[r] = spread(s_strip[r] + next_slot(s_strip[r]), False)

    at_cut = lane == (width - 1) * other

    def mend(value, strip_value, p):
        turn = (-(16 * (p + 2) + 8)) % width
        turned = pltpu.roll(strip_value, turn, 1) if turn else strip_value
        return jnp.where(at_cut, turned, value)

    z_share = jnp.where(last_row, 1.0, 0.5)
    yz_share = z_share * jnp.where(jnp.logical_and(last_lane, gy == n_gy - 1), 1.0, 0.5)
    share = [yz_share * 0.5] * planes
    share[planes - 1] = jnp.where(has_right, share[0], yz_share)

    def mend_w(p):
        for c in range(3):
            w_ref[p + 1, c] = mend(w_ref[p + 1, c], strip_w[c], p)

    def put_stress(ref, p, parts, strip_ref):
        for r in range(6):
            value = spread(parts[p, r] + parts[p + 1, r], True)
            ref[p, r] = mend(value, strip_ref[r], p) * share[p]

    sums = [zero] * 3 + [jnp.zeros((8, width), jnp.float32)]

    def modes_of_w(p):
        keep_modes(wm_ref, p, [w_ref[p + 1, c] for c in range(3)])

    def w_element(p):
        def body(tile, total):
            fields, scale = tile_fields(wm_ref, p, tile), tile_scale(p, tile)
            keep_stress(swe_ref, p, tile, fields, scale)
            return total + energy(fields, scale) if p < planes else total

        sums[3] = tiles(body, sums[3])

    def add_sums(p):
        for c in range(3):
            b, w = b_ref[p, c], w_ref[p + 1, c]
            sums[0] = sums[0] + b * b
            sums[1] = sums[1] + b * w
            sums[2] = sums[2] + w * w

    fields = strip_fields(strip_w)
    s_strip = stresses(fields, strip_e)
    counted = jnp.logical_and(lax.rem(lane, 16) == 8, jnp.logical_and(lane >= 32, lane < 32 + 16 * planes))
    counted = jnp.logical_and(counted, gy == 1)
    strip_energy = jnp.where(counted, energy(fields, strip_e), 0.0)
    for r in range(6):
        ssw_ref[r] = spread(s_strip[r] + next_slot(s_strip[r]), False)

    for p in range(1, planes - 1):
        mend_w(p)
        add_sums(p)
        modes_of_w(p)
    for p in range(2, planes - 1):
        w_element(p)
    for p in range(1, planes - 1):
        put_stress(sb_ref, p, sbe_ref, ssb_ref)

    arrived([B_RIGHT], [B_LEFT, E_LEFT])
    keep_b_modes(-1)
    keep_b_modes(planes)
    do_element(0)
    do_element(planes)
    for p in (0, planes - 1):
        raw_w(p)
        mend_w(p)
        add_sums(p)
        modes_of_w(p)
    w_element(1)
    w_element(planes - 1)
    for c in range(3):
        w_ref[0, c] = back(kept(low_ref, 0, c), True)
        w_ref[planes + 1, c] = back(kept(high_ref, planes, c), True)
    for p in (0, planes - 1):
        put_stress(sb_ref, p, sbe_ref, ssb_ref)
    for p in range(1, planes - 1):
        put_stress(sw_ref, p, swe_ref, ssw_ref)

    arrived([P_RIGHT], [])
    for c in range(3):
        w_ref[0, c] = jnp.where(gx == 0, 0.0, pp[c] + w_ref[0, c])
    mend_w(-1)
    modes_of_w(-1)
    w_element(0)
    first = jnp.logical_and(lax.broadcasted_iota(jnp.int32, (8, width), 1) == 0, gy == 1)
    sums[3] = jnp.where(first, 0.0, sums[3])
    for t in range(depth // 8):
        sums[3] = sums[3] + strip_energy[8 * t : 8 * t + 8]

    row8 = lax.broadcasted_iota(jnp.int32, (8, width), 0)
    partial = jnp.zeros((8, width), jnp.float32)
    for k, total in enumerate(sums):
        partial = jnp.where(row8 == k, jnp.sum(total, axis=0, keepdims=True), partial)
    red[...] = partial

    def send_sum(k):
        pltpu.make_async_remote_copy(
            src_ref=red, dst_ref=slots.at[k - 1], send_sem=red_send, recv_sem=red_recv,
            device_id=member(k), device_id_type=MESH).start()

    each_member(send_sum)

    put_stress(sw_ref, 0, swe_ref, ssw_ref)
    arrived([], [Q_LEFT])
    for c in range(3):
        w_ref[planes + 1, c] = qq[c] + w_ref[planes + 1, c]
    mend_w(planes)
    modes_of_w(planes)
    w_element(planes)
    put_stress(sw_ref, planes - 1, swe_ref, ssw_ref)

    pltpu.make_async_copy(slots, slots, red_recv).wait()
    total = red[...]
    if n <= 32:
        for k in range(n - 1):
            total = total + slots[k]
    else:
        total = lax.fori_loop(0, n - 1, lambda k, value: value + slots[k], total)
    whole = jnp.broadcast_to(jnp.sum(total, axis=1, keepdims=True), (8, width))
    bb, bw, ww, wkw = (whole[k : k + 1] for k in range(4))
    first_step = bb / bw
    norm = bb - 2.0 * first_step * bw + first_step * first_step * ww
    ratio = norm / bb
    grown = 1.0 + ratio
    curve = grown * grown * bw - 2.0 * grown * first_step * ww + first_step * first_step * wkw
    second_step = norm / curve
    on_b = first_step + second_step * grown
    on_w = -second_step * first_step
    for p in range(planes):
        for c in range(3):
            x_out[c, pl.ds(p, depth, stride=planes), :] = on_b * b_ref[p, c] + on_w * w_ref[p + 1, c]
        for r in range(6):
            s_out[r, pl.ds(p, depth, stride=planes), :] = on_b * sb_ref[p, r] + on_w * sw_ref[p, r]

    to_other.wait_send()
    pltpu.make_async_copy(slots, slots, red_send).wait()

    @pl.when(has_right)
    def _():
        for copy in to_right.values():
            copy.wait_send()

    @pl.when(has_left)
    def _():
        for copy in to_left.values():
            copy.wait_send()


def solution(mesh):
    n_gx, n_gy = mesh.shape["gx"], mesh.shape["gy"]

    def per_device(body_force, modulus):
        depth, planes, width = modulus.shape
        assert n_gy == 2 and planes == 4 and width == 128
        rows = depth * planes
        n = n_gx * n_gy
        plane = (depth, width)
        vmem = lambda *dims: pltpu.VMEM(dims, jnp.float32)
        field, stress = pl.pallas_call(
            functools.partial(kernel, n_gx, n_gy),
            out_shape=(
                jax.ShapeDtypeStruct((3, rows, width), jnp.float32),
                jax.ShapeDtypeStruct((6, rows, width), jnp.float32),
            ),
            in_specs=[pl.BlockSpec(memory_space=pltpu.HBM)] * 2,
            out_specs=(pl.BlockSpec(memory_space=pltpu.VMEM),) * 2,
            scratch_shapes=[
                vmem(3, rows, width),
                vmem(rows, width),
                vmem(planes, 3, *plane),
                vmem(planes, *plane),
                vmem(3, *plane),
                vmem(3, *plane),
                vmem(3, *plane),
                vmem(*plane),
                vmem(3, *plane),
                vmem(3, *plane),
                vmem(3, *plane),
                vmem(2, *plane),
                vmem(2, *plane),
                vmem(4, *plane),
                vmem(planes + 2, 3, *plane),
                vmem(planes + 2, 12, *plane),
                vmem(planes + 2, 12, *plane),
                vmem(planes + 1, 12, *plane),
                vmem(planes + 1, 12, *plane),
                vmem(planes + 1, 6, *plane),
                vmem(planes + 1, 6, *plane),
                vmem(planes, 6, *plane),
                vmem(planes, 6, *plane),
                vmem(6, *plane),
                vmem(6, *plane),
                vmem(8, width),
                vmem(n - 1, 8, width),
                pltpu.SemaphoreType.DMA((2,)),
                pltpu.SemaphoreType.DMA((10,)),
                pltpu.SemaphoreType.DMA((10,)),
                pltpu.SemaphoreType.DMA,
                pltpu.SemaphoreType.DMA,
            ],
            compiler_params=pltpu.CompilerParams(
                collective_id=0, has_side_effects=True, vmem_limit_bytes=32 * 1024 * 1024
            ),
        )(
            pltpu.with_memory_space_constraint(body_force.reshape(3, rows, width), pltpu.HBM),
            pltpu.with_memory_space_constraint(modulus.reshape(rows, width), pltpu.HBM),
        )
        return (
            field.reshape(3, depth, planes, width),
            stress.reshape(6, depth, planes, width),
        )

    return jax.shard_map(
        per_device,
        mesh=mesh,
        in_specs=(P(None, "sample", "gx", "gy"), P("sample", "gx", "gy")),
        out_specs=(P(None, "sample", "gx", "gy"), P(None, "sample", "gx", "gy")),
        check_vma=False,
    )
```

```python
import functools
import math

import jax
import jax.numpy as jnp
import numpy as np
from jax import lax
from jax.experimental import pallas as pl
from jax.experimental.pallas import tpu as pltpu
from jax.sharding import PartitionSpec as P

MESH = pl.DeviceIdType.MESH


def corner_list():
    return [(off_z, off_x, off_y) for off_z in (0, 1) for off_x in (0, 1) for off_y in (0, 1)]


def strain_matrix(point):
    corners = corner_list()
    grads = np.zeros((3, 8))
    for corner, offsets in enumerate(corners):
        for axis in range(3):
            value = 1.0 if offsets[axis] else -1.0
            for other in range(3):
                if other != axis:
                    value = value * (point[other] if offsets[other] else 1.0 - point[other])
            grads[axis, corner] = value
    strain = np.zeros((6, 24))
    for corner in range(8):
        for axis in range(3):
            strain[axis, axis * 8 + corner] = grads[axis, corner]
        strain[3, 0 * 8 + corner] = grads[1, corner]
        strain[3, 1 * 8 + corner] = grads[0, corner]
        strain[4, 1 * 8 + corner] = grads[2, corner]
        strain[4, 2 * 8 + corner] = grads[1, corner]
        strain[5, 0 * 8 + corner] = grads[2, corner]
        strain[5, 2 * 8 + corner] = grads[0, corner]
    return strain


def modal_tables():
    poisson = 0.3
    lame_first = poisson / ((1.0 + poisson) * (1.0 - 2.0 * poisson))
    shear_mod = 1.0 / (2.0 * (1.0 + poisson))
    elastic = np.zeros((6, 6))
    elastic[:3, :3] = lame_first
    for axis in range(3):
        elastic[axis, axis] += 2.0 * shear_mod
        elastic[axis + 3, axis + 3] = shear_mod
    gauss_pts = [0.5 - 0.5 / math.sqrt(3.0), 0.5 + 0.5 / math.sqrt(3.0)]
    stiffness = np.zeros((24, 24))
    for first in gauss_pts:
        for second in gauss_pts:
            for third in gauss_pts:
                strain = strain_matrix((first, second, third))
                stiffness += strain.T @ elastic @ strain / 8.0
    stress_map = elastic @ strain_matrix((0.5, 0.5, 0.5))
    pair = np.array([[1.0, 1.0], [-1.0, 1.0]])
    modes = np.kron(np.eye(3), np.kron(pair, np.kron(pair, pair)))
    stiffness = modes @ stiffness @ modes.T / 64.0
    stress_map = stress_map @ modes.T / 8.0

    def rows_of(matrix):
        out = []
        for row in matrix:
            terms = [(q // 8, (q % 8) // 4, (q % 4) // 2, q % 2, float(v)) for q, v in enumerate(row) if abs(v) > 1e-9]
            out.append(terms)
        return out

    return rows_of(stiffness), rows_of(stress_map)


STIFF, STRESS = modal_tables()
B_RIGHT, P_RIGHT, S_RIGHT, D_RIGHT, B_LEFT, E_LEFT, Q_LEFT, S_LEFT, D_LEFT, S_OTHER = range(10)


def combine(terms, fields):
    total = None
    for c, a, b, d, value in terms:
        part = fields[c][a, b, d] * np.float32(value)
        total = part if total is None else total + part
    return total


def kernel(n_gx, n_gy, f_hbm, e_hbm, x_out, s_out,
           f_in, e_in, b_ref, e_ref, bl, pp, br, er, qq, p_out, q_out,
           msg, st_same, st_other, w_ref, sb_ref, sw_ref, ssb_ref, ssw_ref,
           red, slots, in_sem, send_sem, recv_sem, red_send, red_recv):
    gx, gy = lax.axis_index("gx"), lax.axis_index("gy")
    rows = e_hbm.shape[0]
    planes, depth, width = b_ref.shape[0], b_ref.shape[2], b_ref.shape[3]
    has_left, has_right = gx > 0, gx < n_gx - 1
    other = 1 - gy
    n = n_gx * n_gy
    me = gx * n_gy + gy

    load_f = pltpu.make_async_copy(f_hbm, f_in, in_sem.at[0])
    load_e = pltpu.make_async_copy(e_hbm, e_in, in_sem.at[1])
    load_f.start()
    load_e.start()

    barrier = pltpu.get_barrier_semaphore()

    def member(k):
        target = lax.rem(me + k, n)
        return {"gx": target // n_gy, "gy": lax.rem(target, n_gy)}

    def each_member(body):
        if n <= 32:
            for k in range(1, n):
                body(k)
        else:
            lax.fori_loop(1, n, lambda k, carry: (body(k), carry)[1], 0)

    each_member(lambda k: pl.semaphore_signal(barrier, inc=1, device_id=member(k), device_id_type=MESH))

    shape = (depth, width)
    lane = lax.broadcasted_iota(jnp.int32, shape, 1)
    row = lax.broadcasted_iota(jnp.int32, shape, 0)
    zero = jnp.zeros(shape, jnp.float32)
    first_row, last_row = row == 0, row == depth - 1
    first_lane, last_lane = lane == 0, lane == width - 1

    @pl.when(gx == 0)
    def _():
        bl[...] = jnp.zeros_like(bl)
        pp[...] = jnp.zeros_like(pp)
        st_same[0] = zero
        st_other[0] = zero

    @pl.when(gx == n_gx - 1)
    def _():
        br[...] = jnp.zeros_like(br)
        er[...] = jnp.zeros_like(er)
        qq[...] = jnp.zeros_like(qq)
        st_same[1] = zero
        st_other[3] = zero

    def remote(src, dst, which, x, y):
        return pltpu.make_async_remote_copy(
            src_ref=src, dst_ref=dst, send_sem=send_sem.at[which], recv_sem=recv_sem.at[which],
            device_id={"gx": x, "gy": y}, device_id_type=MESH)

    right, left = lax.rem(gx + 1, n_gx), lax.rem(gx + n_gx - 1, n_gx)
    to_right = {
        B_RIGHT: remote(b_ref.at[planes - 1], bl, B_RIGHT, right, gy),
        P_RIGHT: remote(p_out, pp, P_RIGHT, right, gy),
        S_RIGHT: remote(msg.at[1], st_same.at[0], S_RIGHT, right, gy),
        D_RIGHT: remote(msg.at[1], st_other.at[0], D_RIGHT, right, other),
    }
    to_left = {
        B_LEFT: remote(b_ref.at[0], br, B_LEFT, left, gy),
        E_LEFT: remote(e_ref.at[0], er, E_LEFT, left, gy),
        Q_LEFT: remote(q_out, qq, Q_LEFT, left, gy),
        S_LEFT: remote(msg.at[0], st_same.at[1], S_LEFT, left, gy),
        D_LEFT: remote(msg.at[0], st_other.at[3], D_LEFT, left, other),
    }
    to_other = remote(msg, st_other.at[pl.ds(1, 2)], S_OTHER, gx, other)

    def start(rights, lefts):
        @pl.when(has_right)
        def _():
            for which in rights:
                to_right[which].start()

        @pl.when(has_left)
        def _():
            for which in lefts:
                to_left[which].start()

    def arrived(rights, lefts):
        @pl.when(has_left)
        def _():
            for which in rights:
                to_right[which].wait_recv()

        @pl.when(has_right)
        def _():
            for which in lefts:
                to_left[which].wait_recv()

    def take(p):
        for c in range(3):
            b_ref[p, c] = f_in[c, pl.ds(p, depth, stride=planes), :]
        e_ref[p] = e_in[pl.ds(p, depth, stride=planes), :]

    load_f.wait()
    load_e.wait()
    take(planes - 1)
    take(0)
    pl.semaphore_wait(barrier, n - 1)
    start([B_RIGHT], [B_LEFT, E_LEFT])
    for p in range(1, planes - 1):
        take(p)

    for side in range(2):
        packed = None
        for c in range(4):
            for t in range(2):
                p = 2 * side + t
                value = b_ref[p, c] if c < 3 else e_ref[p]
                turned = pltpu.roll(value, (32 * c + 16 * t + 8) % width, 1)
                packed = turned if packed is None else jnp.where(lane // 16 == 2 * c + t, turned, packed)
        msg[side] = packed
    to_other.start()
    start([S_RIGHT, D_RIGHT], [S_LEFT, D_LEFT])

    def y_below(value, edge):
        value = pltpu.roll(value, 1, 1)
        return jnp.where(first_lane, 0.0, value) if edge else value

    def y_above(value, edge):
        value = pltpu.roll(value, width - 1, 1)
        return jnp.where(last_lane, 0.0, value) if edge else value

    def z_below(value):
        return jnp.where(first_row, 0.0, pltpu.roll(value, 1, 0))

    def z_above(value):
        return jnp.where(last_row, 0.0, pltpu.roll(value, depth - 1, 0))

    def forward(value, edge):
        below = y_below(value, edge)
        out = {}
        for d, part in ((0, value + below), (1, value - below)):
            low = z_below(part)
            out[0, d], out[1, d] = part + low, part - low
        return out

    def pair_up(low, high):
        fields = []
        for c in range(3):
            field = {}
            for key in high[c]:
                a, d = key
                field[a, 0, d] = high[c][key] + low[c][key]
                field[a, 1, d] = high[c][key] - low[c][key]
            fields.append(field)
        return fields

    def forces(fields, scale):
        highs, lows = [], []
        for c in range(3):
            high, low = {}, {}
            for a in range(2):
                for d in range(2):
                    diff = combine(STIFF[c * 8 + 4 * a + 2 + d], fields) * scale
                    terms = STIFF[c * 8 + 4 * a + d]
                    if terms:
                        same = combine(terms, fields) * scale
                        high[a, d], low[a, d] = same + diff, same - diff
                    else:
                        high[a, d], low[a, d] = diff, -diff
            highs.append(high)
            lows.append(low)
        return highs, lows

    def back(modes, edge):
        parts = []
        for d in range(2):
            parts.append(modes[0, d] + modes[1, d] + z_above(modes[0, d] - modes[1, d]))
        return parts[0] + parts[1] + y_above(parts[0] - parts[1], edge)

    def add(first, second):
        return {key: first[key] + second[key] for key in first}

    def energy(fields, scale):
        total = None
        for c in range(3):
            for k in range(1, 8):
                part = combine(STIFF[c * 8 + k], fields) * fields[c][k // 4, (k % 4) // 2, k % 2]
                total = part if total is None else total + part
        return total * scale

    def stresses(fields, scale):
        return [combine(STRESS[r], fields) * scale for r in range(6)]

    def spread(value, edge):
        value = value + z_above(value)
        return value + y_above(value, edge)

    def b_plane(p, c):
        return bl[c] if p < 0 else br[c] if p >= planes else b_ref[p, c]

    def b_modes(p):
        return [forward(b_plane(p, c), True) for c in range(3)]

    m2 = [b_modes(p) for p in range(planes)]
    highs, lows, s_b = {}, {}, {}

    def do_element(p, low, high):
        scale = er[...] if p >= planes else e_ref[p]
        fields = pair_up(low, high)
        highs[p], lows[p] = forces(fields, scale)
        s_b[p] = stresses(fields, scale)

    do_element(planes - 1, m2[planes - 2], m2[planes - 1])
    for c in range(3):
        p_out[c] = back(highs[planes - 1][c], True)
    do_element(1, m2[0], m2[1])
    for c in range(3):
        q_out[c] = back(lows[1][c], True)
    start([P_RIGHT], [Q_LEFT])
    for p in range(2, planes - 1):
        do_element(p, m2[p - 1], m2[p])

    def raw_w(p):
        for c in range(3):
            w_ref[p + 1, c] = back(add(highs[p][c], lows[p + 1][c]), True)

    for p in range(1, planes - 1):
        raw_w(p)

    to_other.wait_recv()
    arrived([S_RIGHT, D_RIGHT], [S_LEFT, D_LEFT])
    mine = lax.rem(lane, 16) // 8 == gy
    quarters = [
        jnp.where(mine, st_same[0], st_other[0]),
        jnp.where(mine, msg[0], st_other[1]),
        jnp.where(mine, msg[1], st_other[2]),
        jnp.where(mine, st_same[1], st_other[3]),
    ]
    strip = []
    for c in range(4):
        total = None
        for q in range(4):
            turn = (32 * (q - c)) % width
            turned = pltpu.roll(quarters[q], turn, 1) if turn else quarters[q]
            total = turned if total is None else jnp.where(lane // 32 == q, turned, total)
        strip.append(total)
    strip_e = strip[3]

    def strip_fields(values):
        high = [forward(value, False) for value in values]
        low = [{key: pltpu.roll(field[key], 16, 1) for key in field} for field in high]
        return pair_up(low, high)

    def next_slot(value):
        return pltpu.roll(value, width - 16, 1)

    fields = strip_fields(strip[:3])
    strip_high, strip_low = forces(fields, strip_e)
    s_strip = stresses(fields, strip_e)
    clamped = jnp.logical_and(gx == 0, lane < 32)
    strip_w = []
    for c in range(3):
        modes = {key: strip_high[c][key] + next_slot(strip_low[c][key]) for key in strip_high[c]}
        strip_w.append(jnp.where(clamped, 0.0, back(modes, False)))
    for r in range(6):
        ssb_ref[r] = spread(s_strip[r] + next_slot(s_strip[r]), False)

    at_cut = lane == (width - 1) * other

    def mend(value, strip_value, p):
        turn = (-(16 * (p + 2) + 8)) % width
        turned = pltpu.roll(strip_value, turn, 1) if turn else strip_value
        return jnp.where(at_cut, turned, value)

    z_share = jnp.where(last_row, 1.0, 0.5)
    yz_share = z_share * jnp.where(jnp.logical_and(last_lane, gy == n_gy - 1), 1.0, 0.5)
    share = [yz_share * 0.5] * planes
    share[planes - 1] = jnp.where(has_right, share[0], yz_share)

    def mend_w(p):
        for c in range(3):
            w_ref[p + 1, c] = mend(w_ref[p + 1, c], strip_w[c], p)

    def put_stress(ref, p, below, above, strip_ref):
        for r in range(6):
            value = spread(below[r] + above[r], True)
            ref[p, r] = mend(value, strip_ref[r], p) * share[p]

    s_w, w_modes = {}, {}
    sums = [zero] * 4

    def modes_of_w(p):
        w_modes[p] = [forward(w_ref[p + 1, c], True) for c in range(3)]

    def w_element(p):
        scale = er[...] if p >= planes else e_ref[p]
        fields = pair_up(w_modes[p - 1], w_modes[p])
        if p < planes:
            sums[3] = sums[3] + energy(fields, scale)
        s_w[p] = stresses(fields, scale)

    def add_sums(p):
        for c in range(3):
            b, w = b_ref[p, c], w_ref[p + 1, c]
            sums[0] = sums[0] + b * b
            sums[1] = sums[1] + b * w
            sums[2] = sums[2] + w * w

    fields = strip_fields(strip_w)
    s_strip = stresses(fields, strip_e)
    counted = jnp.logical_and(lax.rem(lane, 16) == 8, jnp.logical_and(lane >= 32, lane < 32 + 16 * planes))
    counted = jnp.logical_and(counted, gy == 1)
    strip_energy = jnp.where(counted, energy(fields, strip_e), 0.0)
    for r in range(6):
        ssw_ref[r] = spread(s_strip[r] + next_slot(s_strip[r]), False)

    for p in range(1, planes - 1):
        mend_w(p)
        add_sums(p)
        modes_of_w(p)
    for p in range(2, planes - 1):
        w_element(p)
    for p in range(1, planes - 1):
        put_stress(sb_ref, p, s_b[p], s_b[p + 1], ssb_ref)

    arrived([B_RIGHT], [B_LEFT, E_LEFT])
    do_element(0, b_modes(-1), m2[0])
    do_element(planes, m2[planes - 1], b_modes(planes))
    for p in (0, planes - 1):
        raw_w(p)
        mend_w(p)
        add_sums(p)
        modes_of_w(p)
    w_element(1)
    w_element(planes - 1)
    for c in range(3):
        w_ref[0, c] = back(lows[0][c], True)
        w_ref[planes + 1, c] = back(highs[planes][c], True)
    for p in (0, planes - 1):
        put_stress(sb_ref, p, s_b[p], s_b[p + 1], ssb_ref)
    for p in range(1, planes - 1):
        put_stress(sw_ref, p, s_w[p], s_w[p + 1], ssw_ref)

    arrived([P_RIGHT], [])
    for c in range(3):
        w_ref[0, c] = jnp.where(gx == 0, 0.0, pp[c] + w_ref[0, c])
    mend_w(-1)
    modes_of_w(-1)
    w_element(0)
    sums[3] = jnp.where(jnp.logical_and(first_lane, gy == 1), 0.0, sums[3]) + strip_energy

    row8 = lax.broadcasted_iota(jnp.int32, (8, width), 0)
    partial = jnp.zeros((8, width), jnp.float32)
    for k, total in enumerate(sums):
        partial = jnp.where(row8 == k, jnp.sum(total, axis=0, keepdims=True), partial)
    red[...] = partial

    def send_sum(k):
        pltpu.make_async_remote_copy(
            src_ref=red, dst_ref=slots.at[k - 1], send_sem=red_send, recv_sem=red_recv,
            device_id=member(k), device_id_type=MESH).start()

    each_member(send_sum)

    put_stress(sw_ref, 0, s_w[0], s_w[1], ssw_ref)
    arrived([], [Q_LEFT])
    for c in range(3):
        w_ref[planes + 1, c] = qq[c] + w_ref[planes + 1, c]
    mend_w(planes)
    modes_of_w(planes)
    w_element(planes)
    put_stress(sw_ref, planes - 1, s_w[planes - 1], s_w[planes], ssw_ref)

    pltpu.make_async_copy(slots, slots, red_recv).wait()
    total = red[...]
    if n <= 32:
        for k in range(n - 1):
            total = total + slots[k]
    else:
        total = lax.fori_loop(0, n - 1, lambda k, value: value + slots[k], total)
    whole = jnp.broadcast_to(jnp.sum(total, axis=1, keepdims=True), (8, width))
    bb, bw, ww, wkw = (whole[k : k + 1] for k in range(4))
    first_step = bb / bw
    norm = bb - 2.0 * first_step * bw + first_step * first_step * ww
    ratio = norm / bb
    grown = 1.0 + ratio
    curve = grown * grown * bw - 2.0 * grown * first_step * ww + first_step * first_step * wkw
    second_step = norm / curve
    on_b = first_step + second_step * grown
    on_w = -second_step * first_step
    for p in range(planes):
        for c in range(3):
            x_out[c, pl.ds(p, depth, stride=planes), :] = on_b * b_ref[p, c] + on_w * w_ref[p + 1, c]
        for r in range(6):
            s_out[r, pl.ds(p, depth, stride=planes), :] = on_b * sb_ref[p, r] + on_w * sw_ref[p, r]

    to_other.wait_send()
    pltpu.make_async_copy(slots, slots, red_send).wait()

    @pl.when(has_right)
    def _():
        for copy in to_right.values():
            copy.wait_send()

    @pl.when(has_left)
    def _():
        for copy in to_left.values():
            copy.wait_send()


def store(x_ref, s_ref, x_out, s_out, sem):
    copies = [
        pltpu.make_async_copy(s_ref, s_out, sem.at[1]),
        pltpu.make_async_copy(x_ref, x_out, sem.at[0]),
    ]
    for copy in copies:
        copy.start()
    for copy in copies:
        copy.wait()


def solution(mesh):
    n_gx, n_gy = mesh.shape["gx"], mesh.shape["gy"]

    def per_device(body_force, modulus):
        depth, planes, width = modulus.shape
        assert n_gy == 2 and planes == 4 and width == 128
        rows = depth * planes
        n = n_gx * n_gy
        plane = (depth, width)
        vmem = lambda *dims: pltpu.VMEM(dims, jnp.float32)
        field, stress = pl.pallas_call(
            functools.partial(kernel, n_gx, n_gy),
            out_shape=(
                jax.ShapeDtypeStruct((3, rows, width), jnp.float32),
                jax.ShapeDtypeStruct((6, rows, width), jnp.float32),
            ),
            in_specs=[pl.BlockSpec(memory_space=pltpu.HBM)] * 2,
            out_specs=(pl.BlockSpec(memory_space=pltpu.VMEM),) * 2,
            scratch_shapes=[
                vmem(3, rows, width),
                vmem(rows, width),
                vmem(planes, 3, *plane),
                vmem(planes, *plane),
                vmem(3, *plane),
                vmem(3, *plane),
                vmem(3, *plane),
                vmem(*plane),
                vmem(3, *plane),
                vmem(3, *plane),
                vmem(3, *plane),
                vmem(2, *plane),
                vmem(2, *plane),
                vmem(4, *plane),
                vmem(planes + 2, 3, *plane),
                vmem(planes, 6, *plane),
                vmem(planes, 6, *plane),
                vmem(6, *plane),
                vmem(6, *plane),
                vmem(8, width),
                vmem(n - 1, 8, width),
                pltpu.SemaphoreType.DMA((2,)),
                pltpu.SemaphoreType.DMA((10,)),
                pltpu.SemaphoreType.DMA((10,)),
                pltpu.SemaphoreType.DMA,
                pltpu.SemaphoreType.DMA,
            ],
            compiler_params=pltpu.CompilerParams(
                collective_id=0, has_side_effects=True, vmem_limit_bytes=32 * 1024 * 1024
            ),
        )(
            pltpu.with_memory_space_constraint(body_force.reshape(3, rows, width), pltpu.HBM),
            pltpu.with_memory_space_constraint(modulus.reshape(rows, width), pltpu.HBM),
        )
        field, stress = pl.pallas_call(
            store,
            out_shape=(
                jax.ShapeDtypeStruct((3, rows, width), jnp.float32),
                jax.ShapeDtypeStruct((6, rows, width), jnp.float32),
            ),
            in_specs=[pl.BlockSpec(memory_space=pl.ANY)] * 2,
            out_specs=(pl.BlockSpec(memory_space=pltpu.HBM),) * 2,
            scratch_shapes=[pltpu.SemaphoreType.DMA((2,))],
            compiler_params=pltpu.CompilerParams(vmem_limit_bytes=4 * 1024 * 1024),
        )(field, stress)
        return (
            field.reshape(3, depth, planes, width),
            stress.reshape(6, depth, planes, width),
        )

    return jax.shard_map(
        per_device,
        mesh=mesh,
        in_specs=(P(None, "sample", "gx", "gy"), P("sample", "gx", "gy")),
        out_specs=(P(None, "sample", "gx", "gy"), P(None, "sample", "gx", "gy")),
        check_vma=False,
    )
```
